256 devices in a mesh: samples: 32 (over z, x_lo, core), mp: 8 (over y, x_hi).
Axes of the slice: x: 4 (x_hi: 2, x_lo: 2; x = x_hi * 2 + x_lo), y: 4, z: 8, core: 2. Of those that a mesh axis runs over, the one named last changes fastest.
Arguments:
- spin_values: int32 [128, 256], P('samples'), may hold values from -1 to 1, as said below
- features: bfloat16 [128, 256, 1024], P('samples'), may hold values from -6 to 6
- spin_embed: bfloat16 [1024], replicated, may hold values from -4 to 4
- norm_gain: bfloat16 [1024], replicated, may hold values from 0.25 to 1.75
- up_weight: bfloat16 [1024, 4096], P(None, 'mp'), may hold values from -0.1875 to 0.1875
- down_weight: bfloat16 [1024, 4096], P(None, 'mp'), may hold values from -0.09375 to 0.09375
- readout: bfloat16 [1024], replicated, may hold values from -0.00012207031 to 0.00012207031
- local_energy: float32 [128], P('samples'), may hold values from -60 to 60
- damping: float32 [1], replicated, may hold values from 7.1525574e-06 to 7.1525574e-05
Outputs:
- solution: float32 [1024, 4096], P('samples', 'mp')
The draws below stay inside these ranges and needn't reach their ends.
Inputs may be any that keep to these rules, and one draw needn't show every extreme that they name: `spin_values`: every entry is -1 or +1.
All inputs are finite; a program needn't handle non-finite values.
Results may differ from the reference program's by a relative error of at most 0.0073.
Values may be sent and summed in bfloat16 or wider, within the bound.
No kernel may reach another device: no remote copies, remote signals or barrier semaphores. Data moves between devices by JAX's collectives and lax.ppermute only.
A program may use at most 64 MiB of HBM per device.

```python
import math
import jax
import jax.numpy as jnp
from jax import lax

D = 1024
FF = 4096
L = 256
ITERS = 3
SAMPLES = 128


def draw_spin_values(key, part):
    key = jax.random.fold_in(key, 7)
    spin_bits = jax.random.randint(key, (SAMPLES, L), 0, 2)
    return (2 * spin_bits - 1).astype(jnp.int32)


def shard_levels(own_key, shape, shards, smallest, top_value):
    gain = 1.0
    for dim, parts in shards:
        heights = jax.random.uniform(jax.random.fold_in(jax.random.fold_in(own_key, 6), dim), (parts,), jnp.float32, smallest / len(shards), top_value / len(shards))
        gain = gain * jnp.repeat(jnp.exp(heights), shape[dim] // parts).reshape((-1,) + (1,) * (len(shape) - 1 - dim))
    return gain


def normal_values(key, shape, scale, reach, cuts=(), dtype=jnp.bfloat16):
    values = jax.random.normal(key, shape, jnp.float32) * scale
    if len(cuts) > 0:
        values = shard_levels(key, shape, cuts, -0.22, 0.18) * values
    return jnp.clip(values, min=-reach, max=reach).astype(dtype)


def setup_inputs(seed: int = 0) -> dict:
    streams_of = jax.random.split(jax.random.key(seed), 10)
    return {
        "spin_values": draw_spin_values(jax.random.fold_in(streams_of[9], 71), 0),
        "features": normal_values(streams_of[1], (SAMPLES, L, D), 1.0, 6.0, ((0, 32),)),
        "spin_embed": normal_values(streams_of[2], (D,), 0.5, 4.0),
        "norm_gain": jnp.clip(1.0 + 0.15 * jax.random.normal(streams_of[3], (D,), jnp.float32), 0.25, 1.75).astype(jnp.bfloat16),
        "up_weight": normal_values(streams_of[4], (D, FF), D ** -0.5, 0.1875, ((1, 8),)),
        "down_weight": normal_values(streams_of[5], (D, FF), FF ** -0.5, 0.09375, ((1, 8),)),
        "readout": normal_values(streams_of[6], (D,), (48 * SAMPLES ** 0.5 * L ** -0.5 * (D * FF) ** -1), 0.00012207031),
        "local_energy": normal_values(streams_of[7], (SAMPLES,), 10.0, 60.0, ((0, 32),), jnp.float32),
        "damping": jnp.clip(jnp.exp(jax.random.uniform(streams_of[8], (1,), jnp.float32, math.log(7.152557373046875e-06), math.log(7.152557373046875e-05))), 7.152557373046875e-06, 7.152557373046875e-05),
    }


gelu_coef = 0.7978845608028654
cubic_coef = 0.044715

def gelu_value(value_in):
    return 0.5 * value_in * (1.0 + jnp.tanh(gelu_coef * (value_in + cubic_coef * value_in * value_in * value_in)))

def gelu_slope(value_in):
    inner_tanh = jnp.tanh(gelu_coef * (value_in + cubic_coef * value_in * value_in * value_in))
    return 0.5 * (1.0 + inner_tanh) + 0.5 * value_in * (1.0 - inner_tanh * inner_tanh) * gelu_coef * (1.0 + 3.0 * cubic_coef * value_in * value_in)

def linearize(sample_items, spin_embed, norm_gain, up_weight, down_weight, readout):
    sample_features, sample_spins = sample_items
    inputs = sample_features.astype(jnp.float32) + sample_spins.astype(jnp.float32)[:, None] * spin_embed.astype(jnp.float32)[None, :]
    inv_scale = lax.rsqrt(lax.optimization_barrier(jnp.mean(inputs * inputs, axis=1, keepdims=True)) + 1e-05)
    normed = (inputs * inv_scale * norm_gain.astype(jnp.float32)).astype(jnp.bfloat16)
    hidden_pre = jnp.dot(normed, up_weight, preferred_element_type=jnp.float32)
    activated = gelu_value(hidden_pre).astype(jnp.bfloat16)
    mixed_rows = lax.dot_general(activated, down_weight, (((1,), (1,)), ((), ())), preferred_element_type=jnp.float32)
    outputs = inputs + mixed_rows
    slope_all = (readout.astype(jnp.float32) * jnp.tanh(outputs)).astype(jnp.bfloat16)
    back_proj = jnp.dot(slope_all, down_weight, preferred_element_type=jnp.float32)
    pullback = (gelu_slope(hidden_pre) * back_proj).astype(jnp.bfloat16)
    return (normed, pullback)

def gradient_sum(normed, pullback, weights):

    def add_one(running, sample_items):
        row_block, pull_rows, weight = sample_items
        scaled = (pull_rows.astype(jnp.float32) * weight).astype(jnp.bfloat16)
        return (running + lax.dot_general(row_block, scaled, (((0,), (0,)), ((), ())), preferred_element_type=jnp.float32), None)
    start_sum = jnp.zeros((normed.shape[2], pullback.shape[2]), jnp.float32)
    running, unused = lax.scan(add_one, start_sum, (normed, pullback, weights))
    return running

def reference(spin_values, features, spin_embed, norm_gain, up_weight, down_weight, readout, local_energy, damping):

    def one_sample(sample_items):
        return linearize(sample_items, spin_embed, norm_gain, up_weight, down_weight, readout)
    normed, pullback = lax.map(one_sample, (features, spin_values))
    sample_count = local_energy.shape[0]
    energy_mean = jnp.sum(local_energy) / sample_count
    force = gradient_sum(normed, pullback, (local_energy - energy_mean) / sample_count)
    solution = jnp.zeros_like(force)
    residual = force
    direction = force
    norm_now = jnp.sum(residual * residual)
    for iteration in range(ITERS):
        direction_half = direction.astype(jnp.bfloat16)

        def value_of(sample_items):
            projected = jnp.dot(sample_items[0], direction_half, preferred_element_type=jnp.float32)
            return jnp.sum(projected * sample_items[1].astype(jnp.float32))
        values = lax.map(value_of, (normed, pullback))
        value_mean = jnp.sum(values) / sample_count
        image = gradient_sum(normed, pullback, (values - value_mean) / sample_count) + damping[0] * direction
        step_size = norm_now / jnp.sum(direction * image)
        solution = solution + step_size * direction
        residual = residual - step_size * image
        norm_next = jnp.sum(residual * residual)
        direction = residual + norm_next / norm_now * direction
        norm_now = norm_next
    return solution
```

```python
import jax
import jax.numpy as jnp
from jax import lax
from jax.experimental import pallas as pl
from jax.experimental.pallas import tpu as pltpu
from jax.sharding import PartitionSpec as P

ITERS = 3


gelu_coef = 0.7978845608028654
cubic_coef = 0.044715


def gelu_value(value_in):
    return (
        0.5
        * value_in
        * (1.0 + jnp.tanh(gelu_coef * (value_in + cubic_coef * value_in * value_in * value_in)))
    )


def gelu_slope(value_in):
    inner_tanh = jnp.tanh(gelu_coef * (value_in + cubic_coef * value_in * value_in * value_in))
    return 0.5 * (1.0 + inner_tanh) + 0.5 * value_in * (
        1.0 - inner_tanh * inner_tanh
    ) * gelu_coef * (1.0 + 3.0 * cubic_coef * value_in * value_in)


def encode(value):
    square = value * value
    return jnp.where(value < 0, -square * square, square * square).astype(jnp.bfloat16)


def decode(code):
    code = code.astype(jnp.float32)
    root = lax.rsqrt(lax.rsqrt(jnp.abs(code)))
    root = jnp.where(code == 0, 0.0, root)
    return jnp.where(code < 0, -root, root)


def share(array, axis):
    size = lax.axis_size(axis)
    return lax.all_to_all(jnp.broadcast_to(array, (size,) + array.shape), axis, 0, 0)


def solve_kernel(gram_ref, energy_row_ref, energy_col_ref, damping_ref, coef_ref):
    count = gram_ref.shape[0]
    gram = gram_ref[...]
    gram = gram - jnp.sum(gram, axis=1, keepdims=True) / count
    gram = gram - jnp.sum(gram, axis=0, keepdims=True) / count
    damping = damping_ref[0]

    def center(row, col):
        return (
            (row - jnp.sum(row, axis=1, keepdims=True) / count) / count,
            (col - jnp.sum(col, axis=0, keepdims=True) / count) / count,
        )

    def apply(row, col):
        return jnp.sum(gram * col, axis=0, keepdims=True), jnp.sum(gram * row, axis=1, keepdims=True)

    def inner(row, other):
        return jnp.sum(row * other, axis=1, keepdims=True)

    residual = center(energy_row_ref[...], energy_col_ref[...])
    direction = residual
    solution = jnp.zeros_like(residual[1])
    norm_now = inner(residual[0], apply(*residual)[0])
    for _ in range(ITERS):
        values = apply(*direction)
        weights = center(*values)
        image = tuple(w + damping * d for w, d in zip(weights, direction))
        step_size = norm_now / inner(values[0], image[0])
        solution = solution + step_size * direction[1]
        residual = tuple(r - step_size * i for r, i in zip(residual, image))
        norm_next = inner(residual[0], apply(*residual)[0])
        ratio = norm_next / norm_now
        direction = tuple(r + ratio * d for r, d in zip(residual, direction))
        norm_now = norm_next
    coef_ref[...] = solution


def solve(gram, energy, damping):
    count = energy.shape[0]
    vmem = pl.BlockSpec(memory_space=pltpu.VMEM)
    return pl.pallas_call(
        solve_kernel,
        out_shape=jax.ShapeDtypeStruct((count, 1), jnp.float32),
        in_specs=[vmem, vmem, vmem, pl.BlockSpec(memory_space=pltpu.SMEM)],
        out_specs=vmem,
    )(gram, energy.reshape(1, count), energy.reshape(count, 1), damping)


def body(
    spin_values,
    features,
    spin_embed,
    norm_gain,
    up_weight,
    down_weight,
    readout,
    local_energy,
    damping,
):
    samp_dev, length, model_width = features.shape
    hidden_dev = up_weight.shape[1]
    tokens = samp_dev * length
    samp_size = lax.axis_size("samples")
    mp_size = lax.axis_size("mp")
    sample_count = samp_dev * samp_size
    rows_dev = model_width // samp_size
    share_rows = tokens // mp_size
    with jax.named_scope("forward"):
        inputs = (
            features.astype(jnp.float32)
            + spin_values.astype(jnp.float32)[:, :, None] * spin_embed.astype(jnp.float32)
        ).reshape(tokens, model_width)
        inv_scale = lax.rsqrt(jnp.mean(inputs * inputs, axis=1, keepdims=True) + 1e-05)
        normed = (inputs * inv_scale * norm_gain.astype(jnp.float32)).astype(jnp.bfloat16)
        hidden_pre = jnp.dot(normed, up_weight, preferred_element_type=jnp.float32)
        activated = gelu_value(hidden_pre).astype(jnp.bfloat16)
        mixed_part = lax.dot_general(
            activated, down_weight, (((1,), (1,)), ((), ())), preferred_element_type=jnp.float32
        ).astype(jnp.bfloat16)
    with jax.named_scope("mixed_exchange"):
        mixed_parts = lax.all_to_all(
            mixed_part.reshape(mp_size, share_rows, model_width), "mp", 0, 0
        )
    with jax.named_scope("slope"):
        mixed_rows = jnp.sum(mixed_parts.astype(jnp.float32), axis=0)
        own_inputs = lax.dynamic_slice_in_dim(
            inputs, lax.axis_index("mp") * share_rows, share_rows, 0
        )
        slope_rows = (readout.astype(jnp.float32) * jnp.tanh(own_inputs + mixed_rows)).astype(
            jnp.bfloat16
        )
    with jax.named_scope("slope_share"):
        slope_all = share(slope_rows, "mp").reshape(tokens, model_width)
    with jax.named_scope("pullback"):
        back_proj = jnp.dot(slope_all, down_weight, preferred_element_type=jnp.float32)
        pullback = (gelu_slope(hidden_pre) * back_proj).astype(jnp.bfloat16)
    with jax.named_scope("derivatives"):
        unit = jnp.maximum(jnp.max(jnp.abs(readout.astype(jnp.float32))), 1e-30)
        derivs = lax.dot_general(
            normed.reshape(samp_dev, length, model_width),
            pullback.reshape(samp_dev, length, hidden_dev),
            (((1,), (1,)), ((0,), (0,))),
            preferred_element_type=jnp.float32,
        )
        coded = encode(derivs * (1.0 / unit)).reshape(samp_dev, samp_size, rows_dev, hidden_dev)
        coded = jnp.swapaxes(coded, 0, 1)
    with jax.named_scope("derivative_exchange"):
        coded = lax.all_to_all(coded, "samples", 0, 0)
        coded = coded.reshape(sample_count, rows_dev, hidden_dev)
    with jax.named_scope("gram"):
        half = decode(coded).astype(jnp.bfloat16)
        gram_part = lax.dot_general(
            half, half, (((1, 2), (1, 2)), ((), ())), preferred_element_type=jnp.float32
        )
    with jax.named_scope("gram_sum"):
        gram_rows = sample_count // mp_size
        gram_mp = jnp.sum(
            lax.all_to_all(gram_part.reshape(mp_size, gram_rows, sample_count), "mp", 0, 0), axis=0
        )
        energy_row = lax.dynamic_update_slice(
            jnp.zeros((8, sample_count), jnp.float32),
            local_energy.reshape(1, samp_dev),
            (0, lax.axis_index("samples") * samp_dev),
        )
        summed = jnp.sum(share(jnp.concatenate([gram_mp, energy_row], axis=0), "samples"), axis=0)
        energy = summed[gram_rows]
        gram = share(summed[:gram_rows], "mp").reshape(sample_count, sample_count)
    with jax.named_scope("solve"):
        coef = solve(gram * (unit * unit), energy, damping)
    with jax.named_scope("combine"):
        return unit * jnp.sum(coef[:, :, None] * decode(coded), axis=0)


def solution(mesh):
    in_specs = (
        P("samples", None),
        P("samples", None, None),
        P(),
        P(),
        P(None, "mp"),
        P(None, "mp"),
        P(),
        P("samples"),
        P(),
    )
    out_specs = P("samples", "mp")
    return jax.shard_map(body, mesh=mesh, in_specs=in_specs, out_specs=out_specs, check_vma=False)
```

```python
import jax
import jax.numpy as jnp
from jax import lax
from jax.experimental import pallas as pl
from jax.experimental.pallas import tpu as pltpu
from jax.sharding import PartitionSpec as P

ITERS = 3
CHUNKS = (2, 2)
VMEM_LIMIT = 60 * 1024 * 1024
VMEM_SMALL = 32 * 1024 * 1024
SAMPLES = ("z", "x_lo", "core")
MP = ("y", "x_hi")
NEAR = ("x_lo", "core", "y")
FAR = ("z", "x_hi")


gelu_coef = 0.7978845608028654
cubic_coef = 0.044715


def encode(value):
    square = value * value
    return jnp.where(value < 0, -square * square, square * square).astype(jnp.bfloat16)


def decode(code):
    code = code.astype(jnp.float32)
    root = lax.rsqrt(lax.rsqrt(jnp.abs(code)))
    root = jnp.where(code == 0, 0.0, root)
    return jnp.where(code < 0, -root, root)


def share(array, axis):
    size = lax.axis_size(axis)
    return lax.all_to_all(jnp.broadcast_to(array, (size,) + array.shape), axis, 0, 0)


VMEM = pl.BlockSpec(memory_space=pltpu.VMEM)
SMEM = pl.BlockSpec(memory_space=pltpu.SMEM)


def forward_kernel(scalar_ref, spin_ref, feature_ref, embed_ref, gain_ref, up_ref, down_ref, *refs):
    normed_ref, own_ref, bend_ref, *part_refs = refs
    blocks, rows, width = feature_ref.shape[1:]
    order = scalar_ref[0]
    own_block = jnp.bitwise_xor(order, scalar_ref[1])
    spin_row = spin_ref[pl.ds(scalar_ref[2] + pl.program_id(0), 1)].astype(jnp.float32)
    offset = lax.broadcasted_iota(jnp.int32, (rows, blocks * rows), 1) - lax.broadcasted_iota(
        jnp.int32, (rows, blocks * rows), 0
    )
    embed = embed_ref[...].astype(jnp.float32).reshape(1, width)
    gain = gain_ref[...].astype(jnp.float32).reshape(1, width)

    def block_inputs(block):
        spin_col = jnp.sum(jnp.where(offset == block * rows, spin_row, 0.0), axis=1, keepdims=True)
        return feature_ref[0, block].astype(jnp.float32) + spin_col * embed

    own_ref[0] = block_inputs(scalar_ref[1])
    for k in range(blocks):
        inputs = block_inputs(jnp.bitwise_xor(order, k))
        inv_scale = lax.rsqrt(jnp.mean(inputs * inputs, axis=1, keepdims=True) + 1e-05)
        normed_ref[0, k * rows : (k + 1) * rows] = (inputs * inv_scale * gain).astype(jnp.bfloat16)
    hidden_pre = jnp.dot(normed_ref[0], up_ref[...], preferred_element_type=jnp.float32)
    square = hidden_pre * hidden_pre
    inner_tanh = jnp.tanh(gelu_coef * (hidden_pre + cubic_coef * square * hidden_pre))
    activated = (0.5 * hidden_pre * (1.0 + inner_tanh)).astype(jnp.bfloat16)
    bend_ref[0] = 0.5 * (1.0 + inner_tanh) + 0.5 * hidden_pre * (
        1.0 - inner_tanh * inner_tanh
    ) * gelu_coef * (1.0 + 3.0 * cubic_coef * square)
    mixed = lax.dot_general(
        activated, down_ref[...], (((1,), (1,)), ((), ())), preferred_element_type=jnp.float32
    ).astype(jnp.bfloat16)
    for k in range(blocks):
        part = mixed[k * rows : (k + 1) * rows]
        if len(part_refs) == 1:
            part_refs[0][k, 0] = part
        else:
            part_refs[k][0] = part


def forward(order, own, spins, features, embed, gain, up, down, first, samples, apart):
    _, blocks, rows, width = features.shape
    hidden = up.shape[1]
    tokens = blocks * rows
    whole = lambda array: pl.BlockSpec(array.shape, lambda s: (0,) * array.ndim)
    block = lambda *shape: pl.BlockSpec((1,) + shape, lambda s: (s,) + (0,) * len(shape))
    result = lambda dtype, *shape: jax.ShapeDtypeStruct((samples,) + shape, dtype)
    if not apart:
        part_specs = [pl.BlockSpec((blocks, 1, rows, width), lambda s: (0, s, 0, 0))]
        part_shapes = [jax.ShapeDtypeStruct((blocks, samples, rows, width), jnp.bfloat16)]
    else:
        part_specs = [block(rows, width)] * blocks
        part_shapes = [result(jnp.bfloat16, rows, width)] * blocks
    scalars = jnp.stack([order, own, jnp.int32(first)])
    return pl.pallas_call(
        forward_kernel,
        grid=(samples,),
        in_specs=[
            SMEM,
            whole(spins),
            pl.BlockSpec((1, blocks, rows, width), lambda s: (s + first, 0, 0, 0)),
            whole(embed),
            whole(gain),
            whole(up),
            whole(down),
        ],
        out_specs=[block(tokens, width), block(rows, width), block(tokens, hidden)] + part_specs,
        out_shape=[
            result(jnp.bfloat16, tokens, width),
            result(jnp.float32, rows, width),
            result(jnp.float32, tokens, hidden),
        ]
        + part_shapes,
        compiler_params=pltpu.CompilerParams(vmem_limit_bytes=VMEM_LIMIT if first == 0 else VMEM_SMALL),
    )(scalars, spins, features, embed, gain, up, down)


def slope_kernel(part_ref, own_ref, readout_ref, *refs):
    slope_ref = refs[-1]
    blocks, samples, rows, width = part_ref.shape
    readout = readout_ref[...].astype(jnp.float32).reshape(1, width)
    for s in range(samples):
        outputs = own_ref[s]
        for k in range(blocks):
            outputs = outputs + part_ref[k, s].astype(jnp.float32)
        slope = (readout * jnp.tanh(outputs)).astype(jnp.bfloat16)
        for k in range(blocks):
            slope_ref[k, s] = slope


def own_slope(parts, own, readout, after):
    return pl.pallas_call(
        slope_kernel,
        out_shape=jax.ShapeDtypeStruct(parts.shape, parts.dtype),
        in_specs=[VMEM] * 3 + [pl.BlockSpec(memory_space=pl.ANY)] * len(after),
        out_specs=VMEM,
        compiler_params=pltpu.CompilerParams(vmem_limit_bytes=VMEM_SMALL),
    )(parts, own, readout, *after)


def derivative_kernel(scale_ref, normed_ref, bend_ref, down_ref, *refs):
    slope_refs, coded_ref = refs[:-1], refs[-1]
    tokens, width = normed_ref.shape[1:]
    if len(slope_refs) == 1:
        slope = slope_refs[0][:, 0].reshape(tokens, width)
    else:
        slope = jnp.concatenate([r[0] for r in slope_refs], axis=0)
    back_proj = jnp.dot(slope, down_ref[...], preferred_element_type=jnp.float32)
    pullback = (bend_ref[0] * back_proj).astype(jnp.bfloat16)
    deriv = lax.dot_general(
        normed_ref[0], pullback, (((0,), (0,)), ((), ())), preferred_element_type=jnp.float32
    )
    coded = encode(deriv * scale_ref[0])
    coded_ref[:, 0] = coded.reshape(coded_ref.shape[0], coded_ref.shape[2], coded_ref.shape[3])


def derivative(scale, normed, bend, down, slopes, parts):
    samples, tokens, width = normed.shape
    hidden = down.shape[1]
    block = lambda *shape: pl.BlockSpec((1,) + shape, lambda s: (s,) + (0,) * len(shape))
    return pl.pallas_call(
        derivative_kernel,
        grid=(samples,),
        in_specs=[
            SMEM,
            block(tokens, width),
            block(tokens, hidden),
            pl.BlockSpec(down.shape, lambda s: (0, 0)),
        ]
        + [
            block(*a.shape[1:])
            if a.ndim == 3
            else pl.BlockSpec((a.shape[0], 1) + a.shape[2:], lambda s: (0, s, 0, 0))
            for a in slopes
        ],
        out_specs=pl.BlockSpec((parts, 1, width // parts, hidden), lambda s: (0, s, 0, 0)),
        out_shape=jax.ShapeDtypeStruct((parts, samples, width // parts, hidden), jnp.bfloat16),
        compiler_params=pltpu.CompilerParams(vmem_limit_bytes=VMEM_SMALL),
    )(scale, normed, bend, down, *slopes)


def widen(code_ref, wide_ref):
    count, rows, lanes = code_ref.shape
    for n in range(0, count, 8):
        wide_ref[0, n * rows : (n + 8) * rows] = decode(code_ref[n : n + 8]).reshape(8 * rows, lanes)


def row_of_all(wide_ref, row, rows):
    count = wide_ref.shape[1] // rows
    return wide_ref[0, pl.ds(row, count, stride=rows)].astype(jnp.bfloat16)


def rows_first_kernel(code_ref, half_ref, wide_ref):
    rows = code_ref.shape[1]
    widen(code_ref, wide_ref)
    for r in range(rows):
        half_ref[r] = row_of_all(wide_ref, r, rows)


LANES = 128


def wide_out(count, rows, width):
    return (
        pl.BlockSpec((1, count * rows, LANES), lambda f: (f, 0, 0)),
        jax.ShapeDtypeStruct((width // LANES, count * rows, LANES), jnp.float32),
    )


def rows_first(code):
    count, rows, width = code.shape
    wide_spec, wide_shape = wide_out(count, rows, width)
    return pl.pallas_call(
        rows_first_kernel,
        grid=(width // LANES,),
        in_specs=[pl.BlockSpec((count, rows, LANES), lambda f: (0, 0, f))],
        out_specs=[pl.BlockSpec((rows, count, LANES), lambda f: (0, 0, f)), wide_spec],
        out_shape=[jax.ShapeDtypeStruct((rows, count, width), jnp.bfloat16), wide_shape],
        compiler_params=pltpu.CompilerParams(vmem_limit_bytes=VMEM_SMALL),
    )(code)


def gram_kernel(energy_ref, code_ref, *refs):
    half_refs, gram_ref, wide_ref = refs[:-2], refs[-2], refs[-1]
    rows = code_ref.shape[1]
    widen(code_ref, wide_ref)
    gram = jnp.zeros(gram_ref.shape, jnp.float32)
    for r in range(0, rows, 4):
        half = jnp.concatenate(
            [
                jnp.concatenate([h[q] for h in half_refs] + [row_of_all(wide_ref, q, rows)], axis=0)
                for q in range(r, r + 4)
            ],
            axis=1,
        )
        gram += lax.dot_general(half, half, (((1,), (1,)), ((), ())), preferred_element_type=jnp.float32)

    @pl.when(pl.program_id(0) == 0)
    def _():
        gram_ref[...] = gram

    @pl.when(pl.program_id(0) > 0)
    def _():
        gram_ref[...] += gram

    @pl.when(pl.program_id(0) == pl.num_programs(0) - 1)
    def _():
        total = gram_ref[...]
        size = total.shape[0]
        row = lax.broadcasted_iota(jnp.int32, total.shape, 0)
        col = lax.broadcasted_iota(jnp.int32, total.shape, 1)
        energy = energy_ref[...]
        total = jnp.where((row == size - 1) & (col < size - 1), energy, total)
        last_energy = jnp.sum(jnp.where(col[:1] == size - 1, energy, 0.0), axis=1, keepdims=True)
        gram_ref[...] = jnp.where((row == size - 2) & (col == 0), last_energy, total)


def gram_matrix(energy, code, halves):
    count, rows, width = code.shape
    size = energy.shape[1]
    wide_spec, wide_shape = wide_out(count, rows, width)
    return pl.pallas_call(
        gram_kernel,
        grid=(width // LANES,),
        in_specs=[
            pl.BlockSpec(energy.shape, lambda f: (0, 0)),
            pl.BlockSpec((count, rows, LANES), lambda f: (0, 0, f)),
        ]
        + [pl.BlockSpec(h.shape[:2] + (LANES,), lambda f: (0, 0, f)) for h in halves],
        out_specs=[pl.BlockSpec((size, size), lambda f: (0, 0)), wide_spec],
        out_shape=[jax.ShapeDtypeStruct((size, size), jnp.float32), wide_shape],
        compiler_params=pltpu.CompilerParams(vmem_limit_bytes=VMEM_LIMIT),
    )(energy, code, *halves)


def solve_kernel(scalar_ref, shared_ref, *refs):
    chunk_count = (len(refs) - 4) // 2
    far_refs, out_ref, gram_ref, spread_ref = refs[:chunk_count], *refs[chunk_count : chunk_count + 3]
    chunk_refs, sems = refs[chunk_count + 3 : -1], refs[-1]
    copies = [
        pltpu.make_async_copy(far, near, sems.at[n])
        for n, (far, near) in enumerate(zip(far_refs, chunk_refs))
    ]
    for copy in copies:
        copy.start()
    count = gram_ref.shape[0]
    gram_rows = shared_ref.shape[1]
    damping, unit = scalar_ref[0], scalar_ref[1]
    for device in range(shared_ref.shape[0]):
        gram_ref[device * gram_rows : (device + 1) * gram_rows] = shared_ref[device]
    row = lax.broadcasted_iota(jnp.int32, (count, count), 0)
    col = lax.broadcasted_iota(jnp.int32, (count, count), 1)
    gram = gram_ref[...]
    energy_row = jnp.where(
        col[:1] == count - 1, gram_ref[count - 2 : count - 1, 0:1], gram_ref[count - 1 : count]
    )
    energy_col = jnp.sum(jnp.where(row == col, energy_row, 0.0), axis=1, keepdims=True)
    gram = jnp.where(row <= col, gram, gram.T) * (unit * unit)
    gram = gram - jnp.sum(gram, axis=1, keepdims=True) / count
    gram = gram - jnp.sum(gram, axis=0, keepdims=True) / count

    def center(row, col):
        return (
            (row - jnp.sum(row, axis=1, keepdims=True) / count) / count,
            (col - jnp.sum(col, axis=0, keepdims=True) / count) / count,
        )

    def apply(row, col):
        return jnp.sum(gram * col, axis=0, keepdims=True), jnp.sum(gram * row, axis=1, keepdims=True)

    def inner(row, other):
        return jnp.sum(row * other, axis=1, keepdims=True)

    residual = center(energy_row, energy_col)
    direction = residual
    coef = jnp.zeros_like(residual[1])
    norm_now = inner(residual[0], apply(*residual)[0])
    for iteration in range(ITERS):
        values = apply(*direction)
        weights = center(*values)
        image = tuple(w + damping * d for w, d in zip(weights, direction))
        step_size = norm_now / inner(values[0], image[0])
        coef = coef + step_size * direction[1]
        if iteration < ITERS - 1:
            residual = tuple(r - step_size * i for r, i in zip(residual, image))
            norm_next = inner(residual[0], apply(*residual)[0])
            ratio = norm_next / norm_now
            direction = tuple(r + ratio * d for r, d in zip(residual, direction))
            norm_now = norm_next
    spread_ref[...] = jnp.broadcast_to(coef * unit, spread_ref.shape)
    for copy in copies:
        copy.wait()
    rows, width = out_ref.shape
    lanes = spread_ref.shape[1]
    for f in range(width // lanes):
        total = jnp.zeros((rows, lanes), jnp.float32)
        first = 0
        for chunk_ref in chunk_refs:
            samples = chunk_ref.shape[1] // rows

            def add(s, total):
                start = pl.multiple_of(s * rows, rows)
                return total + spread_ref[pl.ds(first + s, 1)] * chunk_ref[f, pl.ds(start, rows)]

            total = lax.fori_loop(0, samples, add, total, unroll=8)
            first += samples
        out_ref[:, f * lanes : (f + 1) * lanes] = total


def solve(scalars, shared, chunks, rows):
    count = shared.shape[2]
    return pl.pallas_call(
        solve_kernel,
        out_shape=jax.ShapeDtypeStruct((rows, chunks[0].shape[0] * chunks[0].shape[2]), jnp.float32),
        in_specs=[SMEM, VMEM] + [pl.BlockSpec(memory_space=pl.ANY)] * len(chunks),
        out_specs=VMEM,
        scratch_shapes=[
            pltpu.VMEM((count, count), jnp.float32),
            pltpu.VMEM((count, LANES), jnp.float32),
        ]
        + [pltpu.VMEM(c.shape, c.dtype) for c in chunks]
        + [pltpu.SemaphoreType.DMA((len(chunks),))],
        compiler_params=pltpu.CompilerParams(vmem_limit_bytes=VMEM_LIMIT),
    )(scalars, shared, *chunks)


def body(
    spin_values,
    features,
    spin_embed,
    norm_gain,
    up_weight,
    down_weight,
    readout,
    local_energy,
    damping,
):
    samp_dev, length, model_width = features.shape
    hidden_dev = up_weight.shape[1]
    samp_size = lax.axis_size(SAMPLES)
    mp_size = lax.axis_size(MP)
    sample_count = samp_dev * samp_size
    rows_dev = model_width // samp_size
    share_rows = length // mp_size
    place = lax.axis_index(MP).astype(jnp.int32)
    readout_wide = readout.astype(jnp.float32)
    unit = jnp.maximum(jnp.max(jnp.abs(readout_wide)), 1e-30).reshape(1)
    feature_blocks = features.reshape(samp_dev, mp_size, share_rows, model_width)

    def partner(array, k):
        return lax.ppermute(array, MP, [(i, i ^ k) for i in range(mp_size)])

    with jax.named_scope("energy"):
        energy_row = jnp.zeros((1, sample_count), jnp.float32)
        first = 0
        for samples in CHUNKS:
            energy_row = lax.dynamic_update_slice(
                energy_row,
                local_energy[first : first + samples].reshape(1, samples),
                (0, first * samp_size + lax.axis_index(SAMPLES) * samples),
            )
            first += samples
        energy_row = jnp.where(place == 0, energy_row, 0.0)

    states = []
    first = 0
    for n, samples in enumerate(CHUNKS):
        with jax.named_scope("forward"):
            states.append(
                forward(
                    place if n else jnp.int32(0),
                    place,
                    spin_values,
                    feature_blocks,
                    spin_embed,
                    norm_gain,
                    up_weight,
                    down_weight,
                    first,
                    samples,
                    n > 0,
                )
            )
        first += samples
    coded_chunks = []
    for n, (normed, own_inputs, bend, *parts) in enumerate(states):
        with jax.named_scope("mixed_exchange"):
            if n == 0:
                mixed_parts = lax.all_to_all(parts[0], MP, 0, 0)
            else:
                mixed_parts = parts[:1] + [partner(parts[k], k) for k in range(1, mp_size)]
        with jax.named_scope("slope"):
            if n == 0:
                slope = own_slope(mixed_parts, own_inputs, readout, [s[1] for s in states[1:2]])
            else:
                outputs = own_inputs
                for part in mixed_parts:
                    outputs = outputs + part.astype(jnp.float32)
                slope = (readout_wide * jnp.tanh(outputs)).astype(jnp.bfloat16)
        with jax.named_scope("slope_share"):
            if n == 0:
                slopes = [lax.all_to_all(slope, MP, 0, 0)]
            else:
                slopes = [slope] + [partner(slope, k) for k in range(1, mp_size)]
        with jax.named_scope("derivatives"):
            coded_chunks.append(
                derivative(1.0 / unit, normed, bend, down_weight, slopes, samp_size)
            )
    with jax.named_scope("derivative_exchange"):
        chunks = [lax.all_to_all(c, SAMPLES, 0, 0) for c in coded_chunks]
        chunks = [c.reshape(-1, rows_dev, hidden_dev) for c in chunks]
    with jax.named_scope("gram"):
        halves, wides = zip(*[rows_first(c) for c in chunks[:-1]])
        gram_part, last_wide = gram_matrix(energy_row, chunks[-1], halves)
        wides = wides + (last_wide,)
    with jax.named_scope("gram_sum"):
        near_size = lax.axis_size(NEAR)
        blocks = lax.all_to_all(
            gram_part.reshape(near_size, sample_count // near_size, sample_count), NEAR, 0, 0
        )
        blocks = share(jnp.sum(blocks, axis=0), FAR)
        shared = share(jnp.sum(blocks, axis=0), NEAR)
    with jax.named_scope("solve"):
        return solve(jnp.concatenate([damping, unit]), shared, wides, rows_dev)


def solution(mesh):
    samples, mp = mesh.devices.shape
    fine = jax.sharding.Mesh(
        mesh.devices.reshape(samples // 4, 2, 2, mp // 2, 2), SAMPLES + MP
    )
    in_specs = (
        P(SAMPLES, None),
        P(SAMPLES, None, None),
        P(),
        P(),
        P(None, MP),
        P(None, MP),
        P(),
        P(SAMPLES),
        P(),
    )
    out_specs = P(SAMPLES, MP)
    return jax.shard_map(body, mesh=fine, in_specs=in_specs, out_specs=out_specs, check_vma=False)
```

```python
import functools

import jax
import jax.numpy as jnp
from jax import lax
from jax.experimental import pallas as pl
from jax.experimental.pallas import tpu as pltpu
from jax.sharding import PartitionSpec as P

ITERS = 3
CHUNKS = (2, 2)
VMEM_LIMIT = 60 * 1024 * 1024
VMEM_SMALL = 32 * 1024 * 1024
SAMPLES = ("z", "x_lo", "core")
MP = ("y", "x_hi")
NEAR = ("x_lo", "core", "y")
FAR = ("z", "x_hi")


gelu_coef = 0.7978845608028654
cubic_coef = 0.044715


def encode(value):
    square = value * value
    return jnp.where(value < 0, -square * square, square * square).astype(jnp.bfloat16)


def decode(code):
    code = code.astype(jnp.float32)
    root = lax.rsqrt(lax.rsqrt(jnp.abs(code)))
    root = jnp.where(code == 0, 0.0, root)
    return jnp.where(code < 0, -root, root)


def share(array, axis):
    size = lax.axis_size(axis)
    return lax.all_to_all(jnp.broadcast_to(array, (size,) + array.shape), axis, 0, 0)


VMEM = pl.BlockSpec(memory_space=pltpu.VMEM)
SMEM = pl.BlockSpec(memory_space=pltpu.SMEM)


def forward_kernel(scalar_ref, spin_ref, feature_ref, embed_ref, gain_ref, up_ref, down_ref, *refs):
    normed_ref, own_ref, bend_ref, *part_refs = refs
    blocks, rows, width = feature_ref.shape[1:]
    order = scalar_ref[0]
    own_block = jnp.bitwise_xor(order, scalar_ref[1])
    spin_row = spin_ref[pl.ds(scalar_ref[2] + pl.program_id(0), 1)].astype(jnp.float32)
    offset = lax.broadcasted_iota(jnp.int32, (rows, blocks * rows), 1) - lax.broadcasted_iota(
        jnp.int32, (rows, blocks * rows), 0
    )
    embed = embed_ref[...].astype(jnp.float32).reshape(1, width)
    gain = gain_ref[...].astype(jnp.float32).reshape(1, width)

    def block_inputs(block):
        spin_col = jnp.sum(jnp.where(offset == block * rows, spin_row, 0.0), axis=1, keepdims=True)
        return feature_ref[0, block].astype(jnp.float32) + spin_col * embed

    own_ref[0] = block_inputs(scalar_ref[1])
    for k in range(blocks):
        inputs = block_inputs(jnp.bitwise_xor(order, k))
        inv_scale = lax.rsqrt(jnp.mean(inputs * inputs, axis=1, keepdims=True) + 1e-05)
        normed_ref[0, k * rows : (k + 1) * rows] = (inputs * inv_scale * gain).astype(jnp.bfloat16)
    hidden_pre = jnp.dot(normed_ref[0], up_ref[...], preferred_element_type=jnp.float32)
    square = hidden_pre * hidden_pre
    inner_tanh = jnp.tanh(gelu_coef * (hidden_pre + cubic_coef * square * hidden_pre))
    activated = (0.5 * hidden_pre * (1.0 + inner_tanh)).astype(jnp.bfloat16)
    bend_ref[0] = 0.5 * (1.0 + inner_tanh) + 0.5 * hidden_pre * (
        1.0 - inner_tanh * inner_tanh
    ) * gelu_coef * (1.0 + 3.0 * cubic_coef * square)
    mixed = lax.dot_general(
        activated, down_ref[...], (((1,), (1,)), ((), ())), preferred_element_type=jnp.float32
    ).astype(jnp.bfloat16)
    for k in range(blocks):
        part = mixed[k * rows : (k + 1) * rows]
        if len(part_refs) == 1:
            part_refs[0][k, 0] = part
        else:
            part_refs[k][0] = part


def forward(order, own, spins, features, embed, gain, up, down, first, samples, apart):
    _, blocks, rows, width = features.shape
    hidden = up.shape[1]
    tokens = blocks * rows
    whole = lambda array: pl.BlockSpec(array.shape, lambda s: (0,) * array.ndim)
    block = lambda *shape: pl.BlockSpec((1,) + shape, lambda s: (s,) + (0,) * len(shape))
    result = lambda dtype, *shape: jax.ShapeDtypeStruct((samples,) + shape, dtype)
    if not apart:
        part_specs = [pl.BlockSpec((blocks, 1, rows, width), lambda s: (0, s, 0, 0))]
        part_shapes = [jax.ShapeDtypeStruct((blocks, samples, rows, width), jnp.bfloat16)]
    else:
        part_specs = [block(rows, width)] * blocks
        part_shapes = [result(jnp.bfloat16, rows, width)] * blocks
    scalars = jnp.stack([order, own, jnp.int32(first)])
    return pl.pallas_call(
        forward_kernel,
        grid=(samples,),
        in_specs=[
            SMEM,
            whole(spins),
            pl.BlockSpec((1, blocks, rows, width), lambda s: (s + first, 0, 0, 0)),
            whole(embed),
            whole(gain),
            whole(up),
            whole(down),
        ],
        out_specs=[block(tokens, width), block(rows, width), block(tokens, hidden)] + part_specs,
        out_shape=[
            result(jnp.bfloat16, tokens, width),
            result(jnp.float32, rows, width),
            result(jnp.float32, tokens, hidden),
        ]
        + part_shapes,
        compiler_params=pltpu.CompilerParams(vmem_limit_bytes=VMEM_LIMIT),
    )(scalars, spins, features, embed, gain, up, down)


def slope_kernel(part_ref, own_ref, readout_ref, slope_ref):
    blocks, samples, rows, width = part_ref.shape
    readout = readout_ref[...].astype(jnp.float32).reshape(1, width)
    for s in range(samples):
        outputs = own_ref[s]
        for k in range(blocks):
            outputs = outputs + part_ref[k, s].astype(jnp.float32)
        slope = (readout * jnp.tanh(outputs)).astype(jnp.bfloat16)
        for k in range(blocks):
            slope_ref[k, s] = slope


def own_slope(parts, own, readout):
    return pl.pallas_call(
        slope_kernel,
        out_shape=jax.ShapeDtypeStruct(parts.shape, parts.dtype),
        in_specs=[VMEM] * 3,
        out_specs=VMEM,
        compiler_params=pltpu.CompilerParams(vmem_limit_bytes=VMEM_SMALL),
    )(parts, own, readout)


def derivative_kernel(slope_count, scale_ref, normed_ref, bend_ref, down_ref, *refs):
    slope_refs, coded_ref = refs[:slope_count], refs[-1]
    tokens, width = normed_ref.shape[1:]
    if len(slope_refs) == 1:
        slope = slope_refs[0][:, 0].reshape(tokens, width)
    else:
        slope = jnp.concatenate([r[0] for r in slope_refs], axis=0)
    back_proj = jnp.dot(slope, down_ref[...], preferred_element_type=jnp.float32)
    pullback = (bend_ref[0] * back_proj).astype(jnp.bfloat16)
    deriv = lax.dot_general(
        normed_ref[0], pullback, (((0,), (0,)), ((), ())), preferred_element_type=jnp.float32
    )
    coded = encode(deriv * scale_ref[0])
    coded_ref[:, 0] = coded.reshape(coded_ref.shape[0], coded_ref.shape[2], coded_ref.shape[3])


def derivative(scale, normed, bend, down, slopes, parts, after):
    samples, tokens, width = normed.shape
    hidden = down.shape[1]
    block = lambda *shape: pl.BlockSpec((1,) + shape, lambda s: (s,) + (0,) * len(shape))
    return pl.pallas_call(
        functools.partial(derivative_kernel, len(slopes)),
        grid=(samples,),
        in_specs=[
            SMEM,
            block(tokens, width),
            block(tokens, hidden),
            pl.BlockSpec(down.shape, lambda s: (0, 0)),
        ]
        + [
            block(*a.shape[1:])
            if a.ndim == 3
            else pl.BlockSpec((a.shape[0], 1) + a.shape[2:], lambda s: (0, s, 0, 0))
            for a in slopes
        ]
        + [pl.BlockSpec((1, 16, 128), lambda s: (0, 0, 0))] * len(after),
        out_specs=pl.BlockSpec((parts, 1, width // parts, hidden), lambda s: (0, s, 0, 0)),
        out_shape=jax.ShapeDtypeStruct((parts, samples, width // parts, hidden), jnp.bfloat16),
        compiler_params=pltpu.CompilerParams(vmem_limit_bytes=VMEM_SMALL),
    )(scale, normed, bend, down, *slopes, *after)


LANES = 128


def widen(code_ref, wide_ref, apart_ref):
    count, rows, _ = code_ref.shape
    for n in range(count):
        values = decode(code_ref[n])
        wide_ref[0, n * rows : (n + 1) * rows] = values
        apart_ref[n * (rows + 1) : n * (rows + 1) + rows] = values


def row_of_all(apart_ref, row, count, rows):
    return apart_ref[pl.ds(row, count, stride=rows + 1)].astype(jnp.bfloat16)


def apart_scratch(count, rows):
    return pltpu.VMEM((-(-count * (rows + 1) // 8) * 8, LANES), jnp.float32)


def wide_out(count, rows, width):
    return (
        pl.BlockSpec((1, count * rows, LANES), lambda f: (f, 0, 0)),
        pltpu.HBM((width // LANES, count * rows, LANES), jnp.float32),
    )


def rows_first_kernel(code_ref, half_ref, wide_ref, apart_ref):
    count, rows, _ = code_ref.shape
    widen(code_ref, wide_ref, apart_ref)
    for r in range(rows):
        half_ref[r] = row_of_all(apart_ref, r, count, rows)


def rows_first(code):
    count, rows, width = code.shape
    wide_spec, wide_shape = wide_out(count, rows, width)
    return pl.pallas_call(
        rows_first_kernel,
        grid=(width // LANES,),
        in_specs=[pl.BlockSpec((count, rows, LANES), lambda f: (0, 0, f))],
        out_specs=[pl.BlockSpec((rows, count, LANES), lambda f: (0, 0, f)), wide_spec],
        out_shape=[jax.ShapeDtypeStruct((rows, count, width), jnp.bfloat16), wide_shape],
        scratch_shapes=[apart_scratch(count, rows)],
        compiler_params=pltpu.CompilerParams(vmem_limit_bytes=VMEM_LIMIT),
    )(code)


def gram_kernel(energy_ref, code_ref, *refs):
    half_refs, gram_ref, wide_ref, apart_ref = refs[:-3], *refs[-3:]
    count, rows, _ = code_ref.shape
    widen(code_ref, wide_ref, apart_ref)
    gram = jnp.zeros(gram_ref.shape, jnp.float32)
    for r in range(0, rows, 4):
        half = jnp.concatenate(
            [
                jnp.concatenate([h[q] for h in half_refs] + [row_of_all(apart_ref, q, count, rows)], axis=0)
                for q in range(r, r + 4)
            ],
            axis=1,
        )
        gram += lax.dot_general(half, half, (((1,), (1,)), ((), ())), preferred_element_type=jnp.float32)

    @pl.when(pl.program_id(0) == 0)
    def _():
        gram_ref[...] = gram

    @pl.when(pl.program_id(0) > 0)
    def _():
        gram_ref[...] += gram

    @pl.when(pl.program_id(0) == pl.num_programs(0) - 1)
    def _():
        total = gram_ref[...]
        size = total.shape[0]
        row = lax.broadcasted_iota(jnp.int32, total.shape, 0)
        col = lax.broadcasted_iota(jnp.int32, total.shape, 1)
        energy = energy_ref[...]
        total = jnp.where((row == size - 1) & (col < size - 1), energy, total)
        last_energy = jnp.sum(jnp.where(col[:1] == size - 1, energy, 0.0), axis=1, keepdims=True)
        gram_ref[...] = jnp.where((row == size - 2) & (col == 0), last_energy, total)


def gram_matrix(energy, code, halves):
    count, rows, width = code.shape
    size = energy.shape[1]
    wide_spec, wide_shape = wide_out(count, rows, width)
    return pl.pallas_call(
        gram_kernel,
        grid=(width // LANES,),
        in_specs=[
            pl.BlockSpec(energy.shape, lambda f: (0, 0)),
            pl.BlockSpec((count, rows, LANES), lambda f: (0, 0, f)),
        ]
        + [pl.BlockSpec(h.shape[:2] + (LANES,), lambda f: (0, 0, f)) for h in halves],
        out_specs=[pl.BlockSpec((size, size), lambda f: (0, 0)), wide_spec],
        out_shape=[jax.ShapeDtypeStruct((size, size), jnp.float32), wide_shape],
        scratch_shapes=[apart_scratch(count, rows)],
        compiler_params=pltpu.CompilerParams(vmem_limit_bytes=VMEM_SMALL),
    )(energy, code, *halves)


def solve_kernel(scalar_ref, shared_ref, *refs):
    chunk_count = (len(refs) - 4) // 2
    far_refs, out_ref, gram_ref, spread_ref = refs[:chunk_count], *refs[chunk_count : chunk_count + 3]
    chunk_refs, sems = refs[chunk_count + 3 : -1], refs[-1]
    copies = [
        pltpu.make_async_copy(far, near, sems.at[n])
        for n, (far, near) in enumerate(zip(far_refs, chunk_refs))
    ]
    for copy in copies:
        copy.start()
    count = gram_ref.shape[0]
    gram_rows = shared_ref.shape[1]
    damping, unit = scalar_ref[0], scalar_ref[1]
    for device in range(shared_ref.shape[0]):
        gram_ref[device * gram_rows : (device + 1) * gram_rows] = shared_ref[device]
    row = lax.broadcasted_iota(jnp.int32, (count, count), 0)
    col = lax.broadcasted_iota(jnp.int32, (count, count), 1)
    gram = gram_ref[...]
    energy_row = jnp.where(
        col[:1] == count - 1, gram_ref[count - 2 : count - 1, 0:1], gram_ref[count - 1 : count]
    )
    energy_col = jnp.sum(jnp.where(row == col, energy_row, 0.0), axis=1, keepdims=True)
    gram = jnp.where(row <= col, gram, gram.T) * (unit * unit)
    gram = gram - jnp.sum(gram, axis=1, keepdims=True) / count
    gram = gram - jnp.sum(gram, axis=0, keepdims=True) / count

    def center(row, col):
        return (
            (row - jnp.sum(row, axis=1, keepdims=True) / count) / count,
            (col - jnp.sum(col, axis=0, keepdims=True) / count) / count,
        )

    def apply(row, col):
        return jnp.sum(gram * col, axis=0, keepdims=True), jnp.sum(gram * row, axis=1, keepdims=True)

    def inner(row, other):
        return jnp.sum(row * other, axis=1, keepdims=True)

    residual = center(energy_row, energy_col)
    direction = residual
    coef = jnp.zeros_like(residual[1])
    norm_now = inner(residual[0], apply(*residual)[0])
    for iteration in range(ITERS):
        values = apply(*direction)
        weights = center(*values)
        image = tuple(w + damping * d for w, d in zip(weights, direction))
        step_size = norm_now / inner(values[0], image[0])
        coef = coef + step_size * direction[1]
        if iteration < ITERS - 1:
            residual = tuple(r - step_size * i for r, i in zip(residual, image))
            norm_next = inner(residual[0], apply(*residual)[0])
            ratio = norm_next / norm_now
            direction = tuple(r + ratio * d for r, d in zip(residual, direction))
            norm_now = norm_next
    spread_ref[...] = jnp.broadcast_to(coef * unit, spread_ref.shape)
    for copy in copies:
        copy.wait()
    rows, width = out_ref.shape
    lanes = spread_ref.shape[1]
    groups = 2
    for f in range(0, width // lanes, groups):
        total = (jnp.zeros((rows, lanes), jnp.float32),) * groups
        first = 0
        for chunk_ref in chunk_refs:
            samples = chunk_ref.shape[1] // rows

            def add(s, total):
                start = pl.multiple_of(s * rows, rows)
                spread = spread_ref[pl.ds(first + s, 1)]
                return tuple(t + spread * chunk_ref[f + g, pl.ds(start, rows)] for g, t in enumerate(total))

            total = lax.fori_loop(0, samples, add, total, unroll=8)
            first += samples
        for g in range(groups):
            out_ref[:, (f + g) * lanes : (f + g + 1) * lanes] = total[g]


def solve(scalars, shared, chunks, rows):
    count = shared.shape[2]
    return pl.pallas_call(
        solve_kernel,
        out_shape=jax.ShapeDtypeStruct((rows, chunks[0].shape[0] * chunks[0].shape[2]), jnp.float32),
        in_specs=[SMEM, VMEM] + [pl.BlockSpec(memory_space=pltpu.HBM)] * len(chunks),
        out_specs=VMEM,
        scratch_shapes=[
            pltpu.VMEM((count, count), jnp.float32),
            pltpu.VMEM((count, LANES), jnp.float32),
        ]
        + [pltpu.VMEM(c.shape, c.dtype) for c in chunks]
        + [pltpu.SemaphoreType.DMA((len(chunks),))],
        compiler_params=pltpu.CompilerParams(vmem_limit_bytes=VMEM_LIMIT),
    )(scalars, shared, *chunks)


def body(
    spin_values,
    features,
    spin_embed,
    norm_gain,
    up_weight,
    down_weight,
    readout,
    local_energy,
    damping,
):
    samp_dev, length, model_width = features.shape
    hidden_dev = up_weight.shape[1]
    samp_size = lax.axis_size(SAMPLES)
    mp_size = lax.axis_size(MP)
    sample_count = samp_dev * samp_size
    rows_dev = model_width // samp_size
    share_rows = length // mp_size
    place = lax.axis_index(MP).astype(jnp.int32)
    readout_wide = readout.astype(jnp.float32)
    unit = jnp.maximum(jnp.max(jnp.abs(readout_wide)), 1e-30).reshape(1)
    feature_blocks = features.reshape(samp_dev, mp_size, share_rows, model_width)

    def partner(array, k):
        return lax.ppermute(array, MP, [(i, i ^ k) for i in range(mp_size)])

    with jax.named_scope("energy"):
        energy_row = jnp.zeros((1, sample_count), jnp.float32)
        first = 0
        for samples in CHUNKS:
            energy_row = lax.dynamic_update_slice(
                energy_row,
                local_energy[first : first + samples].reshape(1, samples),
                (0, first * samp_size + lax.axis_index(SAMPLES) * samples),
            )
            first += samples
        energy_row = jnp.where(place == 0, energy_row, 0.0)

    states = []
    first = 0
    for n, samples in enumerate(CHUNKS):
        with jax.named_scope("forward"):
            states.append(
                forward(
                    place if n else jnp.int32(0),
                    place,
                    spin_values,
                    feature_blocks,
                    spin_embed,
                    norm_gain,
                    up_weight,
                    down_weight,
                    first,
                    samples,
                    n > 0,
                )
            )
        first += samples
    coded_chunks = []
    for n, (normed, own_inputs, bend, *parts) in enumerate(states):
        with jax.named_scope("mixed_exchange"):
            if n == 0:
                mixed_parts = lax.all_to_all(parts[0], MP, 0, 0)
            else:
                mixed_parts = parts[:1] + [partner(parts[k], k) for k in range(1, mp_size)]
        with jax.named_scope("slope"):
            if n == 0:
                slope = own_slope(mixed_parts, own_inputs, readout)
            else:
                outputs = own_inputs
                for part in mixed_parts:
                    outputs = outputs + part.astype(jnp.float32)
                slope = (readout_wide * jnp.tanh(outputs)).astype(jnp.bfloat16)
        with jax.named_scope("slope_share"):
            if n == 0:
                slopes = [lax.all_to_all(slope, MP, 0, 0)]
            else:
                slopes = [slope] + [partner(slope, k) for k in range(1, mp_size)]
        with jax.named_scope("derivatives"):
            after = [state[3] for state in states[n + 1 : n + 2]]
            coded_chunks.append(
                derivative(1.0 / unit, normed, bend, down_weight, slopes, samp_size, after)
            )
    with jax.named_scope("derivative_exchange"):
        chunks = [lax.all_to_all(c, SAMPLES, 0, 0) for c in coded_chunks]
        chunks = [c.reshape(-1, rows_dev, hidden_dev) for c in chunks]
    with jax.named_scope("gram"):
        halves, wides = zip(*[rows_first(c) for c in chunks[:-1]])
        gram_part, last_wide = gram_matrix(energy_row, chunks[-1], halves)
        wides = wides + (last_wide,)
    with jax.named_scope("gram_sum"):
        near_size = lax.axis_size(NEAR)
        blocks = lax.all_to_all(
            gram_part.reshape(near_size, sample_count // near_size, sample_count), NEAR, 0, 0
        )
        blocks = share(jnp.sum(blocks, axis=0), FAR)
        shared = share(jnp.sum(blocks, axis=0), NEAR)
    with jax.named_scope("solve"):
        return solve(jnp.concatenate([damping, unit]), shared, wides, rows_dev)


def solution(mesh):
    samples, mp = mesh.devices.shape
    fine = jax.sharding.Mesh(
        mesh.devices.reshape(samples // 4, 2, 2, mp // 2, 2), SAMPLES + MP
    )
    in_specs = (
        P(SAMPLES, None),
        P(SAMPLES, None, None),
        P(),
        P(),
        P(None, MP),
        P(None, MP),
        P(),
        P(SAMPLES),
        P(),
    )
    out_specs = P(SAMPLES, MP)
    return jax.shard_map(body, mesh=fine, in_specs=in_specs, out_specs=out_specs, check_vma=False)
```

```python
import functools

import jax
import jax.numpy as jnp
from jax import lax
from jax.experimental import pallas as pl
from jax.experimental.pallas import tpu as pltpu
from jax.sharding import PartitionSpec as P

ITERS = 3
CHUNKS = (2, 2)
VMEM_LIMIT = 60 * 1024 * 1024
VMEM_SMALL = 32 * 1024 * 1024
SAMPLES = ("z", "x_lo", "core")
MP = ("y", "x_hi")
NEAR = ("x_lo", "core", "y")
FAR = ("z", "x_hi")


gelu_coef = 0.7978845608028654
cubic_coef = 0.044715


def encode(value):
    square = value * value
    return jnp.where(value < 0, -square * square, square * square).astype(jnp.bfloat16)


def decode(code):
    code = code.astype(jnp.float32)
    root = lax.rsqrt(lax.rsqrt(jnp.abs(code)))
    root = jnp.where(code == 0, 0.0, root)
    return jnp.where(code < 0, -root, root)


def share(array, axis):
    size = lax.axis_size(axis)
    return lax.all_to_all(jnp.broadcast_to(array, (size,) + array.shape), axis, 0, 0)


VMEM = pl.BlockSpec(memory_space=pltpu.VMEM)
SMEM = pl.BlockSpec(memory_space=pltpu.SMEM)


def forward_kernel(scalar_ref, spin_ref, feature_ref, embed_ref, gain_ref, up_ref, down_ref, *refs):
    normed_ref, own_ref, bend_ref, *part_refs = refs
    blocks, rows, width = feature_ref.shape[1:]
    order = scalar_ref[0]
    own_block = jnp.bitwise_xor(order, scalar_ref[1])
    spin_row = spin_ref[pl.ds(scalar_ref[2] + pl.program_id(0), 1)].astype(jnp.float32)
    offset = lax.broadcasted_iota(jnp.int32, (rows, blocks * rows), 1) - lax.broadcasted_iota(
        jnp.int32, (rows, blocks * rows), 0
    )
    embed = embed_ref[...].astype(jnp.float32).reshape(1, width)
    gain = gain_ref[...].astype(jnp.float32).reshape(1, width)

    def block_inputs(block):
        spin_col = jnp.sum(jnp.where(offset == block * rows, spin_row, 0.0), axis=1, keepdims=True)
        return feature_ref[0, block].astype(jnp.float32) + spin_col * embed

    own_ref[0] = block_inputs(scalar_ref[1])
    for k in range(blocks):
        inputs = block_inputs(jnp.bitwise_xor(order, k))
        inv_scale = lax.rsqrt(jnp.mean(inputs * inputs, axis=1, keepdims=True) + 1e-05)
        normed_ref[0, k * rows : (k + 1) * rows] = (inputs * inv_scale * gain).astype(jnp.bfloat16)
    hidden_pre = jnp.dot(normed_ref[0], up_ref[...], preferred_element_type=jnp.float32)
    square = hidden_pre * hidden_pre
    inner_tanh = jnp.tanh(gelu_coef * (hidden_pre + cubic_coef * square * hidden_pre))
    activated = (0.5 * hidden_pre * (1.0 + inner_tanh)).astype(jnp.bfloat16)
    bend_ref[0] = 0.5 * (1.0 + inner_tanh) + 0.5 * hidden_pre * (
        1.0 - inner_tanh * inner_tanh
    ) * gelu_coef * (1.0 + 3.0 * cubic_coef * square)
    mixed = lax.dot_general(
        activated, down_ref[...], (((1,), (1,)), ((), ())), preferred_element_type=jnp.float32
    ).astype(jnp.bfloat16)
    for k in range(blocks):
        part = mixed[k * rows : (k + 1) * rows]
        per_ref = part_refs[0].shape[0]
        part_refs[k // per_ref][k % per_ref, 0] = part


def forward(order, own, spins, features, embed, gain, up, down, first, samples, pairs):
    _, blocks, rows, width = features.shape
    hidden = up.shape[1]
    tokens = blocks * rows
    whole = lambda array: pl.BlockSpec(array.shape, lambda s: (0,) * array.ndim)
    block = lambda *shape: pl.BlockSpec((1,) + shape, lambda s: (s,) + (0,) * len(shape))
    result = lambda dtype, *shape: jax.ShapeDtypeStruct((samples,) + shape, dtype)
    together = 2 if pairs else blocks
    part_specs = [pl.BlockSpec((together, 1, rows, width), lambda s: (0, s, 0, 0))] * (
        blocks // together
    )
    part_shapes = [jax.ShapeDtypeStruct((together, samples, rows, width), jnp.bfloat16)] * (
        blocks // together
    )
    scalars = jnp.stack([order, own, jnp.int32(first)])
    return pl.pallas_call(
        forward_kernel,
        grid=(samples,),
        in_specs=[
            SMEM,
            whole(spins),
            pl.BlockSpec((1, blocks, rows, width), lambda s: (s + first, 0, 0, 0)),
            whole(embed),
            whole(gain),
            whole(up),
            whole(down),
        ],
        out_specs=[block(tokens, width), block(rows, width), block(tokens, hidden)] + part_specs,
        out_shape=[
            result(jnp.bfloat16, tokens, width),
            result(jnp.float32, rows, width),
            result(jnp.float32, tokens, hidden),
        ]
        + part_shapes,
        compiler_params=pltpu.CompilerParams(vmem_limit_bytes=VMEM_LIMIT),
    )(scalars, spins, features, embed, gain, up, down)


def slope_kernel(part_ref, own_ref, readout_ref, slope_ref):
    blocks, samples, rows, width = part_ref.shape
    readout = readout_ref[...].astype(jnp.float32).reshape(1, width)
    for s in range(samples):
        outputs = own_ref[s]
        for k in range(blocks):
            outputs = outputs + part_ref[k, s].astype(jnp.float32)
        slope = (readout * jnp.tanh(outputs)).astype(jnp.bfloat16)
        for k in range(blocks):
            slope_ref[k, s] = slope


def own_slope(parts, own, readout):
    return pl.pallas_call(
        slope_kernel,
        out_shape=jax.ShapeDtypeStruct(parts.shape, parts.dtype),
        in_specs=[VMEM] * 3,
        out_specs=VMEM,
        compiler_params=pltpu.CompilerParams(vmem_limit_bytes=VMEM_SMALL),
    )(parts, own, readout)


def derivative_kernel(slope_count, scale_ref, normed_ref, bend_ref, down_ref, *refs):
    slope_refs, coded_ref = refs[:slope_count], refs[-1]
    tokens, width = normed_ref.shape[1:]
    slope = jnp.concatenate([r[:, 0].reshape(-1, width) for r in slope_refs], axis=0)
    back_proj = jnp.dot(slope, down_ref[...], preferred_element_type=jnp.float32)
    pullback = (bend_ref[0] * back_proj).astype(jnp.bfloat16)
    deriv = lax.dot_general(
        normed_ref[0], pullback, (((0,), (0,)), ((), ())), preferred_element_type=jnp.float32
    )
    coded = encode(deriv * scale_ref[0])
    coded_ref[:, 0] = coded.reshape(coded_ref.shape[0], coded_ref.shape[2], coded_ref.shape[3])


def derivative(scale, normed, bend, down, slopes, parts, after):
    samples, tokens, width = normed.shape
    hidden = down.shape[1]
    block = lambda *shape: pl.BlockSpec((1,) + shape, lambda s: (s,) + (0,) * len(shape))
    return pl.pallas_call(
        functools.partial(derivative_kernel, len(slopes)),
        grid=(samples,),
        in_specs=[
            SMEM,
            block(tokens, width),
            block(tokens, hidden),
            pl.BlockSpec(down.shape, lambda s: (0, 0)),
        ]
        + [
            pl.BlockSpec((a.shape[0], 1) + a.shape[2:], lambda s: (0, s, 0, 0))
            for a in slopes
        ]
        + [pl.BlockSpec((1, 1, 16, 128), lambda s: (0, 0, 0, 0))] * len(after),
        out_specs=pl.BlockSpec((parts, 1, width // parts, hidden), lambda s: (0, s, 0, 0)),
        out_shape=jax.ShapeDtypeStruct((parts, samples, width // parts, hidden), jnp.bfloat16),
        compiler_params=pltpu.CompilerParams(vmem_limit_bytes=VMEM_SMALL),
    )(scale, normed, bend, down, *slopes, *after)


LANES = 128


def widen(code_ref, wide_ref, apart_ref):
    count, rows, _ = code_ref.shape
    for n in range(count):
        values = decode(code_ref[n])
        wide_ref[0, n * rows : (n + 1) * rows] = values
        apart_ref[n * (rows + 1) : n * (rows + 1) + rows] = values


def row_of_all(apart_ref, row, count, rows):
    return apart_ref[pl.ds(row, count, stride=rows + 1)].astype(jnp.bfloat16)


def apart_scratch(count, rows):
    return pltpu.VMEM((-(-count * (rows + 1) // 8) * 8, LANES), jnp.float32)


def wide_out(count, rows, width):
    return (
        pl.BlockSpec((1, count * rows, LANES), lambda f: (f, 0, 0)),
        pltpu.HBM((width // LANES, count * rows, LANES), jnp.float32),
    )


def rows_first_kernel(code_ref, half_ref, wide_ref, apart_ref):
    count, rows, _ = code_ref.shape
    widen(code_ref, wide_ref, apart_ref)
    for r in range(rows):
        half_ref[r] = row_of_all(apart_ref, r, count, rows)


def rows_first(code):
    count, rows, width = code.shape
    wide_spec, wide_shape = wide_out(count, rows, width)
    return pl.pallas_call(
        rows_first_kernel,
        grid=(width // LANES,),
        in_specs=[pl.BlockSpec((count, rows, LANES), lambda f: (0, 0, f))],
        out_specs=[pl.BlockSpec((rows, count, LANES), lambda f: (0, 0, f)), wide_spec],
        out_shape=[jax.ShapeDtypeStruct((rows, count, width), jnp.bfloat16), wide_shape],
        scratch_shapes=[apart_scratch(count, rows)],
        compiler_params=pltpu.CompilerParams(vmem_limit_bytes=VMEM_LIMIT),
    )(code)


def gram_kernel(energy_ref, code_ref, *refs):
    half_refs, gram_ref, wide_ref, apart_ref = refs[:-3], *refs[-3:]
    count, rows, _ = code_ref.shape
    widen(code_ref, wide_ref, apart_ref)
    gram = jnp.zeros(gram_ref.shape, jnp.float32)
    for r in range(0, rows, 4):
        half = jnp.concatenate(
            [
                jnp.concatenate([h[q] for h in half_refs] + [row_of_all(apart_ref, q, count, rows)], axis=0)
                for q in range(r, r + 4)
            ],
            axis=1,
        )
        gram += lax.dot_general(half, half, (((1,), (1,)), ((), ())), preferred_element_type=jnp.float32)

    @pl.when(pl.program_id(0) == 0)
    def _():
        gram_ref[...] = gram

    @pl.when(pl.program_id(0) > 0)
    def _():
        gram_ref[...] += gram

    @pl.when(pl.program_id(0) == pl.num_programs(0) - 1)
    def _():
        total = gram_ref[...]
        size = total.shape[0]
        row = lax.broadcasted_iota(jnp.int32, total.shape, 0)
        col = lax.broadcasted_iota(jnp.int32, total.shape, 1)
        energy = energy_ref[...]
        total = jnp.where((row == size - 1) & (col < size - 1), energy, total)
        last_energy = jnp.sum(jnp.where(col[:1] == size - 1, energy, 0.0), axis=1, keepdims=True)
        gram_ref[...] = jnp.where((row == size - 2) & (col == 0), last_energy, total)


def gram_matrix(energy, code, halves):
    count, rows, width = code.shape
    size = energy.shape[1]
    wide_spec, wide_shape = wide_out(count, rows, width)
    return pl.pallas_call(
        gram_kernel,
        grid=(width // LANES,),
        in_specs=[
            pl.BlockSpec(energy.shape, lambda f: (0, 0)),
            pl.BlockSpec((count, rows, LANES), lambda f: (0, 0, f)),
        ]
        + [pl.BlockSpec(h.shape[:2] + (LANES,), lambda f: (0, 0, f)) for h in halves],
        out_specs=[pl.BlockSpec((size, size), lambda f: (0, 0)), wide_spec],
        out_shape=[jax.ShapeDtypeStruct((size, size), jnp.float32), wide_shape],
        scratch_shapes=[apart_scratch(count, rows)],
        compiler_params=pltpu.CompilerParams(vmem_limit_bytes=VMEM_SMALL),
    )(energy, code, *halves)


def solve_kernel(scalar_ref, shared_ref, *refs):
    chunk_count = (len(refs) - 4) // 2
    far_refs, out_ref, gram_ref, spread_ref = refs[:chunk_count], *refs[chunk_count : chunk_count + 3]
    chunk_refs, sems = refs[chunk_count + 3 : -1], refs[-1]
    copies = [
        pltpu.make_async_copy(far, near, sems.at[n])
        for n, (far, near) in enumerate(zip(far_refs, chunk_refs))
    ]
    for copy in copies:
        copy.start()
    count = gram_ref.shape[0]
    gram_rows = shared_ref.shape[1]
    damping, unit = scalar_ref[0], scalar_ref[1]
    for device in range(shared_ref.shape[0]):
        gram_ref[device * gram_rows : (device + 1) * gram_rows] = shared_ref[device]
    row = lax.broadcasted_iota(jnp.int32, (count, count), 0)
    col = lax.broadcasted_iota(jnp.int32, (count, count), 1)
    gram = gram_ref[...]
    energy_row = jnp.where(
        col[:1] == count - 1, gram_ref[count - 2 : count - 1, 0:1], gram_ref[count - 1 : count]
    )
    energy_col = jnp.sum(jnp.where(row == col, energy_row, 0.0), axis=1, keepdims=True)
    gram = jnp.where(row <= col, gram, gram.T) * (unit * unit)
    gram = gram - jnp.sum(gram, axis=1, keepdims=True) / count
    gram = gram - jnp.sum(gram, axis=0, keepdims=True) / count

    def center(row, col):
        return (
            (row - jnp.sum(row, axis=1, keepdims=True) / count) / count,
            (col - jnp.sum(col, axis=0, keepdims=True) / count) / count,
        )

    def apply(row, col):
        return jnp.sum(gram * col, axis=0, keepdims=True), jnp.sum(gram * row, axis=1, keepdims=True)

    def inner(row, other):
        return jnp.sum(row * other, axis=1, keepdims=True)

    residual = center(energy_row, energy_col)
    direction = residual
    coef = jnp.zeros_like(residual[1])
    norm_now = inner(residual[0], apply(*residual)[0])
    for iteration in range(ITERS):
        values = apply(*direction)
        weights = center(*values)
        image = tuple(w + damping * d for w, d in zip(weights, direction))
        step_size = norm_now / inner(values[0], image[0])
        coef = coef + step_size * direction[1]
        if iteration < ITERS - 1:
            residual = tuple(r - step_size * i for r, i in zip(residual, image))
            norm_next = inner(residual[0], apply(*residual)[0])
            ratio = norm_next / norm_now
            direction = tuple(r + ratio * d for r, d in zip(residual, direction))
            norm_now = norm_next
    spread_ref[...] = jnp.broadcast_to(coef * unit, spread_ref.shape)
    for copy in copies:
        copy.wait()
    rows, width = out_ref.shape
    lanes = spread_ref.shape[1]
    groups = 2
    for f in range(0, width // lanes, groups):
        total = (jnp.zeros((rows, lanes), jnp.float32),) * groups
        first = 0
        for chunk_ref in chunk_refs:
            samples = chunk_ref.shape[1] // rows

            def add(s, total):
                start = pl.multiple_of(s * rows, rows)
                spread = spread_ref[pl.ds(first + s, 1)]
                return tuple(t + spread * chunk_ref[f + g, pl.ds(start, rows)] for g, t in enumerate(total))

            total = lax.fori_loop(0, samples, add, total, unroll=8)
            first += samples
        for g in range(groups):
            out_ref[:, (f + g) * lanes : (f + g + 1) * lanes] = total[g]


def solve(scalars, shared, chunks, rows):
    count = shared.shape[2]
    return pl.pallas_call(
        solve_kernel,
        out_shape=jax.ShapeDtypeStruct((rows, chunks[0].shape[0] * chunks[0].shape[2]), jnp.float32),
        in_specs=[SMEM, VMEM] + [pl.BlockSpec(memory_space=pltpu.HBM)] * len(chunks),
        out_specs=VMEM,
        scratch_shapes=[
            pltpu.VMEM((count, count), jnp.float32),
            pltpu.VMEM((count, LANES), jnp.float32),
        ]
        + [pltpu.VMEM(c.shape, c.dtype) for c in chunks]
        + [pltpu.SemaphoreType.DMA((len(chunks),))],
        compiler_params=pltpu.CompilerParams(vmem_limit_bytes=VMEM_LIMIT),
    )(scalars, shared, *chunks)


def body(
    spin_values,
    features,
    spin_embed,
    norm_gain,
    up_weight,
    down_weight,
    readout,
    local_energy,
    damping,
):
    samp_dev, length, model_width = features.shape
    hidden_dev = up_weight.shape[1]
    samp_size = lax.axis_size(SAMPLES)
    mp_size = lax.axis_size(MP)
    sample_count = samp_dev * samp_size
    rows_dev = model_width // samp_size
    share_rows = length // mp_size
    place = lax.axis_index(MP).astype(jnp.int32)
    readout_wide = readout.astype(jnp.float32)
    unit = jnp.maximum(jnp.max(jnp.abs(readout_wide)), 1e-30).reshape(1)
    feature_blocks = features.reshape(samp_dev, mp_size, share_rows, model_width)

    def partner(array, k):
        return lax.ppermute(array, MP, [(i, i ^ k) for i in range(mp_size)])

    with jax.named_scope("energy"):
        energy_row = jnp.zeros((1, sample_count), jnp.float32)
        first = 0
        for samples in CHUNKS:
            energy_row = lax.dynamic_update_slice(
                energy_row,
                local_energy[first : first + samples].reshape(1, samples),
                (0, first * samp_size + lax.axis_index(SAMPLES) * samples),
            )
            first += samples
        energy_row = jnp.where(place == 0, energy_row, 0.0)

    states = []
    first = 0
    for n, samples in enumerate(CHUNKS):
        with jax.named_scope("forward"):
            states.append(
                forward(
                    place if n else jnp.int32(0),
                    place,
                    spin_values,
                    feature_blocks,
                    spin_embed,
                    norm_gain,
                    up_weight,
                    down_weight,
                    first,
                    samples,
                    n > 0,
                )
            )
        first += samples
    coded_chunks = []
    for n, (normed, own_inputs, bend, *parts) in enumerate(states):
        with jax.named_scope("mixed_exchange"):
            if n == 0:
                mixed_parts = lax.all_to_all(parts[0], MP, 0, 0)
            else:
                pairs = parts[:1] + [partner(pair, 2 * j) for j, pair in enumerate(parts) if j]
                mixed_own = own_inputs
                mixed_other = 0.0
                for pair in pairs:
                    mixed_own = mixed_own + pair[0].astype(jnp.float32)
                    mixed_other = mixed_other + pair[1].astype(jnp.float32)
                mixed_other = partner(mixed_other.astype(jnp.bfloat16), 1)
        with jax.named_scope("slope"):
            if n == 0:
                slope = own_slope(mixed_parts, own_inputs, readout)
            else:
                outputs = mixed_own + mixed_other.astype(jnp.float32)
                slope = (readout_wide * jnp.tanh(outputs)).astype(jnp.bfloat16)
        with jax.named_scope("slope_share"):
            if n == 0:
                slopes = [lax.all_to_all(slope, MP, 0, 0)]
            else:
                pair = jnp.stack([slope, partner(slope, 1)])
                slopes = [pair] + [partner(pair, 2 * j) for j in range(1, mp_size // 2)]
        with jax.named_scope("derivatives"):
            after = [state[3] for state in states[n + 1 : n + 2]]
            coded_chunks.append(
                derivative(1.0 / unit, normed, bend, down_weight, slopes, samp_size, after)
            )
    with jax.named_scope("derivative_exchange"):
        chunks = [lax.all_to_all(c, SAMPLES, 0, 0) for c in coded_chunks]
        chunks = [c.reshape(-1, rows_dev, hidden_dev) for c in chunks]
    with jax.named_scope("gram"):
        halves, wides = zip(*[rows_first(c) for c in chunks[:-1]])
        gram_part, last_wide = gram_matrix(energy_row, chunks[-1], halves)
        wides = wides + (last_wide,)
    with jax.named_scope("gram_sum"):
        near_size = lax.axis_size(NEAR)
        blocks = lax.all_to_all(
            gram_part.reshape(near_size, sample_count // near_size, sample_count), NEAR, 0, 0
        )
        blocks = share(jnp.sum(blocks, axis=0), FAR)
        shared = share(jnp.sum(blocks, axis=0), NEAR)
    with jax.named_scope("solve"):
        return solve(jnp.concatenate([damping, unit]), shared, wides, rows_dev)


def solution(mesh):
    samples, mp = mesh.devices.shape
    fine = jax.sharding.Mesh(
        mesh.devices.reshape(samples // 4, 2, 2, mp // 2, 2), SAMPLES + MP
    )
    in_specs = (
        P(SAMPLES, None),
        P(SAMPLES, None, None),
        P(),
        P(),
        P(None, MP),
        P(None, MP),
        P(),
        P(SAMPLES),
        P(),
    )
    out_specs = P(SAMPLES, MP)
    return jax.shard_map(body, mesh=fine, in_specs=in_specs, out_specs=out_specs, check_vma=False)
```

```python
import functools

import jax
import jax.numpy as jnp
from jax import lax
from jax.experimental import pallas as pl
from jax.experimental.pallas import tpu as pltpu
from jax.sharding import PartitionSpec as P

ITERS = 3
CHUNKS = (2, 2)
VMEM_LIMIT = 60 * 1024 * 1024
VMEM_SMALL = 32 * 1024 * 1024
SAMPLES = ("z", "x_lo", "core")
MP = ("y", "x_hi")
NEAR = ("z", "core")
FAR = ("x_lo", "y", "x_hi")


gelu_coef = 0.7978845608028654
cubic_coef = 0.044715


def encode(value):
    square = value * value
    return jnp.where(value < 0, -square * square, square * square).astype(jnp.bfloat16)


def decode(code):
    code = code.astype(jnp.float32)
    root = lax.rsqrt(lax.rsqrt(jnp.abs(code)))
    root = jnp.where(code == 0, 0.0, root)
    return jnp.where(code < 0, -root, root)


def share(array, axis):
    size = lax.axis_size(axis)
    return lax.all_to_all(jnp.broadcast_to(array, (size,) + array.shape), axis, 0, 0)


VMEM = pl.BlockSpec(memory_space=pltpu.VMEM)
SMEM = pl.BlockSpec(memory_space=pltpu.SMEM)


def forward_kernel(first, pairs, *refs):
    if pairs:
        order_ref, *refs = refs
        order = order_ref[0]
    spin_ref, feature_ref, embed_ref, gain_ref, up_ref, down_ref, normed_ref, bend_ref, *refs = refs
    blocks, rows, width = feature_ref.shape[1:]
    spin_row = spin_ref[pl.ds(first + pl.program_id(0), 1)].astype(jnp.float32)
    offset = lax.broadcasted_iota(jnp.int32, (rows, blocks * rows), 1) - lax.broadcasted_iota(
        jnp.int32, (rows, blocks * rows), 0
    )
    embed = embed_ref[...].astype(jnp.float32).reshape(1, width)
    gain = gain_ref[...].astype(jnp.float32).reshape(1, width)

    def block_inputs(block):
        spin_col = jnp.sum(jnp.where(offset == block * rows, spin_row, 0.0), axis=1, keepdims=True)
        return feature_ref[0, block].astype(jnp.float32) + spin_col * embed

    part_refs = refs
    if pairs:
        own_ref, mark_ref, *part_refs = refs
        own_ref[0] = block_inputs(order)
        mark_ref[...] = jnp.zeros_like(mark_ref)
    for k in range(blocks):
        inputs = block_inputs(jnp.bitwise_xor(order, k) if pairs else k)
        inv_scale = lax.rsqrt(jnp.mean(inputs * inputs, axis=1, keepdims=True) + 1e-05)
        normed_ref[0, k * rows : (k + 1) * rows] = (inputs * inv_scale * gain).astype(jnp.bfloat16)
    hidden_pre = jnp.dot(normed_ref[0], up_ref[...], preferred_element_type=jnp.float32)
    square = hidden_pre * hidden_pre
    inner_tanh = jnp.tanh(gelu_coef * (hidden_pre + cubic_coef * square * hidden_pre))
    activated = (0.5 * hidden_pre * (1.0 + inner_tanh)).astype(jnp.bfloat16)
    bend_ref[0] = 0.5 * (1.0 + inner_tanh) + 0.5 * hidden_pre * (
        1.0 - inner_tanh * inner_tanh
    ) * gelu_coef * (1.0 + 3.0 * cubic_coef * square)
    mixed = lax.dot_general(
        activated, down_ref[...], (((1,), (1,)), ((), ())), preferred_element_type=jnp.float32
    ).astype(jnp.bfloat16)
    for k in range(blocks):
        part = mixed[k * rows : (k + 1) * rows]
        per_ref = part_refs[0].shape[0]
        part_refs[k // per_ref][k % per_ref, 0] = part


def forward(order, spins, features, embed, gain, up, down, first, samples, pairs):
    _, blocks, rows, width = features.shape
    hidden = up.shape[1]
    tokens = blocks * rows
    whole = lambda array: pl.BlockSpec(array.shape, lambda s: (0,) * array.ndim)
    block = lambda *shape: pl.BlockSpec((1,) + shape, lambda s: (s,) + (0,) * len(shape))
    result = lambda dtype, *shape: jax.ShapeDtypeStruct((samples,) + shape, dtype)
    together = 1 if pairs else blocks
    part_specs = [pl.BlockSpec((together, 1, rows, width), lambda s: (0, s, 0, 0))] * (
        blocks // together
    )
    part_shapes = [jax.ShapeDtypeStruct((together, samples, rows, width), jnp.bfloat16)] * (
        blocks // together
    )
    if pairs:
        part_specs = [block(rows, width), pl.BlockSpec((8, 128), lambda s: (0, 0))] + part_specs
        part_shapes = [
            result(jnp.float32, rows, width),
            jax.ShapeDtypeStruct((8, 128), jnp.float32),
        ] + part_shapes
    return pl.pallas_call(
        functools.partial(forward_kernel, first, pairs),
        grid=(samples,),
        in_specs=[SMEM] * pairs
        + [
            whole(spins),
            pl.BlockSpec((1, blocks, rows, width), lambda s: (s + first, 0, 0, 0)),
            whole(embed),
            whole(gain),
            whole(up),
            whole(down),
        ],
        out_specs=[block(tokens, width), block(tokens, hidden)] + part_specs,
        out_shape=[
            result(jnp.bfloat16, tokens, width),
            result(jnp.float32, tokens, hidden),
        ]
        + part_shapes,
        compiler_params=pltpu.CompilerParams(vmem_limit_bytes=VMEM_LIMIT),
    )(*[order] * pairs, spins, features, embed, gain, up, down)


def slope_kernel(own_ref, part_ref, spin_ref, feature_ref, embed_ref, readout_ref, slope_ref):
    blocks, samples, rows, width = part_ref.shape
    own = own_ref[0]
    offset = lax.broadcasted_iota(jnp.int32, (rows, blocks * rows), 1) - lax.broadcasted_iota(
        jnp.int32, (rows, blocks * rows), 0
    )
    embed = embed_ref[...].astype(jnp.float32).reshape(1, width)
    readout = readout_ref[...].astype(jnp.float32).reshape(1, width)
    for s in range(samples):
        spin_row = spin_ref[s : s + 1].astype(jnp.float32)
        spin_col = jnp.sum(jnp.where(offset == own * rows, spin_row, 0.0), axis=1, keepdims=True)
        outputs = feature_ref[s, own].astype(jnp.float32) + spin_col * embed
        for k in range(blocks):
            outputs = outputs + part_ref[k, s].astype(jnp.float32)
        slope = (readout * jnp.tanh(outputs)).astype(jnp.bfloat16)
        for k in range(blocks):
            slope_ref[k, s] = slope


def own_slope(own, parts, spins, features, embed, readout):
    whole = lambda array: pl.BlockSpec(array.shape, lambda s: (0,) * array.ndim)
    return pl.pallas_call(
        slope_kernel,
        grid=(1,),
        out_shape=pltpu.HBM(parts.shape, parts.dtype),
        in_specs=[
            SMEM,
            whole(parts),
            whole(spins),
            pl.BlockSpec((parts.shape[1],) + features.shape[1:], lambda s: (0, 0, 0, 0)),
            whole(embed),
            whole(readout),
        ],
        out_specs=whole(parts),
        compiler_params=pltpu.CompilerParams(vmem_limit_bytes=VMEM_SMALL),
    )(own, parts, spins, features, embed, readout)


def derivative_kernel(slope_count, scale_ref, normed_ref, bend_ref, down_ref, *refs):
    slope_refs, coded_ref = refs[:slope_count], refs[-1]
    tokens, width = normed_ref.shape[1:]
    slope = jnp.concatenate([r[:, 0].reshape(-1, width) for r in slope_refs], axis=0)
    back_proj = jnp.dot(slope, down_ref[...], preferred_element_type=jnp.float32)
    pullback = (bend_ref[0] * back_proj).astype(jnp.bfloat16)
    deriv = lax.dot_general(
        normed_ref[0], pullback, (((0,), (0,)), ((), ())), preferred_element_type=jnp.float32
    )
    coded = encode(deriv * scale_ref[0])
    coded_ref[:, 0] = coded.reshape(coded_ref.shape[0], coded_ref.shape[2], coded_ref.shape[3])


def derivative(scale, normed, bend, down, slopes, parts, after):
    samples, tokens, width = normed.shape
    hidden = down.shape[1]
    block = lambda *shape: pl.BlockSpec((1,) + shape, lambda s: (s,) + (0,) * len(shape))
    return pl.pallas_call(
        functools.partial(derivative_kernel, len(slopes)),
        grid=(samples,),
        in_specs=[
            SMEM,
            block(tokens, width),
            block(tokens, hidden),
            pl.BlockSpec(down.shape, lambda s: (0, 0)),
        ]
        + [
            pl.BlockSpec((a.shape[0], 1) + a.shape[2:], lambda s: (0, s, 0, 0))
            for a in slopes
        ]
        + [pl.BlockSpec(memory_space=pl.ANY)] * len(after),
        out_specs=pl.BlockSpec((parts, 1, width // parts, hidden), lambda s: (0, s, 0, 0)),
        out_shape=pltpu.HBM((parts, samples, width // parts, hidden), jnp.bfloat16),
        compiler_params=pltpu.CompilerParams(vmem_limit_bytes=VMEM_SMALL),
    )(scale, normed, bend, down, *slopes, *after)


LANES = 128


STEP = 16


def widen(code_ref, wide_ref, apart_ref):
    count, rows, _ = code_ref.shape
    for n in range(count):
        values = decode(code_ref[n])
        for f in range(wide_ref.shape[1]):
            group = values[:, f * LANES : (f + 1) * LANES]
            wide_ref[0, f, n * rows : (n + 1) * rows] = group
            apart_ref[f, n * (rows + 1) : n * (rows + 1) + rows] = group


def row_of_all(apart_ref, row, count, rows):
    groups = [apart_ref[f, pl.ds(row, count, stride=rows + 1)] for f in range(apart_ref.shape[0])]
    return jnp.concatenate(groups, axis=1).astype(jnp.bfloat16)


def apart_scratch(count, width):
    return pltpu.VMEM((width // LANES, -(-count * (STEP + 1) // 8) * 8, LANES), jnp.float32)


def wide_out(count, rows, width):
    return (
        pl.BlockSpec((1, width // LANES, count * STEP, LANES), lambda r: (r, 0, 0, 0)),
        pltpu.HBM((rows // STEP, width // LANES, count * STEP, LANES), jnp.float32),
    )


def rows_first_kernel(code_ref, half_ref, wide_ref, apart_ref):
    count, rows, _ = code_ref.shape
    widen(code_ref, wide_ref, apart_ref)
    for r in range(rows):
        half_ref[r] = row_of_all(apart_ref, r, count, rows)


def rows_first(code):
    count, rows, width = code.shape
    wide_spec, wide_shape = wide_out(count, rows, width)
    return pl.pallas_call(
        rows_first_kernel,
        grid=(rows // STEP,),
        in_specs=[pl.BlockSpec((count, STEP, width), lambda r: (0, r, 0))],
        out_specs=[pl.BlockSpec((STEP, count, width), lambda r: (r, 0, 0)), wide_spec],
        out_shape=[jax.ShapeDtypeStruct((rows, count, width), jnp.bfloat16), wide_shape],
        scratch_shapes=[apart_scratch(count, width)],
        compiler_params=pltpu.CompilerParams(vmem_limit_bytes=VMEM_SMALL),
    )(code)


def gram_kernel(energy_ref, code_ref, *refs):
    half_refs, gram_ref, wide_ref, apart_ref = refs[:-3], *refs[-3:]
    count, rows, _ = code_ref.shape
    widen(code_ref, wide_ref, apart_ref)
    gram = jnp.zeros(gram_ref.shape, jnp.float32)
    for r in range(rows):
        half = jnp.concatenate(
            [h[r] for h in half_refs] + [row_of_all(apart_ref, r, count, rows)], axis=0
        )
        gram += lax.dot_general(half, half, (((1,), (1,)), ((), ())), preferred_element_type=jnp.float32)

    @pl.when(pl.program_id(0) == 0)
    def _():
        gram_ref[...] = gram

    @pl.when(pl.program_id(0) > 0)
    def _():
        gram_ref[...] += gram

    @pl.when(pl.program_id(0) == pl.num_programs(0) - 1)
    def _():
        total = gram_ref[...]
        size = total.shape[0]
        row = lax.broadcasted_iota(jnp.int32, total.shape, 0)
        col = lax.broadcasted_iota(jnp.int32, total.shape, 1)
        energy = energy_ref[...]
        total = jnp.where((row == size - 1) & (col < size - 1), energy, total)
        last_energy = jnp.sum(jnp.where(col[:1] == size - 1, energy, 0.0), axis=1, keepdims=True)
        gram_ref[...] = jnp.where((row == size - 2) & (col == 0), last_energy, total)


def gram_matrix(energy, code, halves):
    count, rows, width = code.shape
    size = energy.shape[1]
    wide_spec, wide_shape = wide_out(count, rows, width)
    return pl.pallas_call(
        gram_kernel,
        grid=(rows // STEP,),
        in_specs=[
            pl.BlockSpec(energy.shape, lambda f: (0, 0)),
            pl.BlockSpec((count, STEP, width), lambda r: (0, r, 0)),
        ]
        + [pl.BlockSpec((STEP,) + h.shape[1:], lambda r: (r, 0, 0)) for h in halves],
        out_specs=[pl.BlockSpec((size, size), lambda f: (0, 0)), wide_spec],
        out_shape=[jax.ShapeDtypeStruct((size, size), jnp.float32), wide_shape],
        scratch_shapes=[apart_scratch(count, width)],
        compiler_params=pltpu.CompilerParams(vmem_limit_bytes=VMEM_LIMIT),
    )(energy, code, *halves)


def solve_kernel(scalar_ref, shared_ref, *refs):
    chunk_count = (len(refs) - 4) // 2
    far_refs, out_ref, gram_ref, spread_ref = refs[:chunk_count], *refs[chunk_count : chunk_count + 3]
    chunk_refs, sems = refs[chunk_count + 3 : -1], refs[-1]
    copies = [
        pltpu.make_async_copy(far, near, sems.at[n])
        for n, (far, near) in enumerate(zip(far_refs, chunk_refs))
    ]
    for copy in copies:
        copy.start()
    count = gram_ref.shape[0]
    gram_rows = shared_ref.shape[1]
    damping, unit = scalar_ref[0], scalar_ref[1]
    for device in range(shared_ref.shape[0]):
        gram_ref[device * gram_rows : (device + 1) * gram_rows] = shared_ref[device]
    row = lax.broadcasted_iota(jnp.int32, (count, count), 0)
    col = lax.broadcasted_iota(jnp.int32, (count, count), 1)
    gram = gram_ref[...]
    energy_row = jnp.where(
        col[:1] == count - 1, gram_ref[count - 2 : count - 1, 0:1], gram_ref[count - 1 : count]
    )
    energy_col = jnp.sum(jnp.where(row == col, energy_row, 0.0), axis=1, keepdims=True)
    gram = jnp.where(row <= col, gram, gram.T) * (unit * unit)
    gram = gram - jnp.sum(gram, axis=1, keepdims=True) / count
    gram = gram - jnp.sum(gram, axis=0, keepdims=True) / count

    def center(row, col):
        return (
            (row - jnp.sum(row, axis=1, keepdims=True) / count) / count,
            (col - jnp.sum(col, axis=0, keepdims=True) / count) / count,
        )

    def apply(row, col):
        return jnp.sum(gram * col, axis=0, keepdims=True), jnp.sum(gram * row, axis=1, keepdims=True)

    def inner(row, other):
        return jnp.sum(row * other, axis=1, keepdims=True)

    residual = center(energy_row, energy_col)
    direction = residual
    coef = jnp.zeros_like(residual[1])
    norm_now = inner(residual[0], apply(*residual)[0])
    for iteration in range(ITERS):
        values = apply(*direction)
        weights = center(*values)
        image = tuple(w + damping * d for w, d in zip(weights, direction))
        step_size = norm_now / inner(values[0], image[0])
        coef = coef + step_size * direction[1]
        if iteration < ITERS - 1:
            residual = tuple(r - step_size * i for r, i in zip(residual, image))
            norm_next = inner(residual[0], apply(*residual)[0])
            ratio = norm_next / norm_now
            direction = tuple(r + ratio * d for r, d in zip(residual, direction))
            norm_now = norm_next
    spread_ref[...] = jnp.broadcast_to(coef * unit, spread_ref.shape)
    lanes = spread_ref.shape[1]
    first = 0
    for n, chunk_ref in enumerate(chunk_refs):
        copies[n].wait()
        steps, groups, depth, _ = chunk_ref.shape
        for r in range(steps):
            here = slice(r * STEP, (r + 1) * STEP)

            def add(s, total):
                start = pl.multiple_of(s * STEP, STEP)
                spread = spread_ref[pl.ds(first + s, 1)]
                return tuple(t + spread * chunk_ref[r, f, pl.ds(start, STEP)] for f, t in enumerate(total))

            total = tuple(
                out_ref[here, f * lanes : (f + 1) * lanes] if n else jnp.zeros((STEP, lanes), jnp.float32)
                for f in range(groups)
            )
            total = lax.fori_loop(0, depth // STEP, add, total, unroll=8)
            for f, t in enumerate(total):
                out_ref[here, f * lanes : (f + 1) * lanes] = t
        first += depth // STEP


def solve(scalars, shared, chunks, rows):
    count = shared.shape[2]
    return pl.pallas_call(
        solve_kernel,
        out_shape=jax.ShapeDtypeStruct((rows, chunks[0].shape[1] * chunks[0].shape[3]), jnp.float32),
        in_specs=[SMEM, VMEM] + [pl.BlockSpec(memory_space=pltpu.HBM)] * len(chunks),
        out_specs=VMEM,
        scratch_shapes=[
            pltpu.VMEM((count, count), jnp.float32),
            pltpu.VMEM((count, LANES), jnp.float32),
        ]
        + [pltpu.VMEM(c.shape, c.dtype) for c in chunks]
        + [pltpu.SemaphoreType.DMA((len(chunks),))],
        compiler_params=pltpu.CompilerParams(vmem_limit_bytes=VMEM_LIMIT),
    )(scalars, shared, *chunks)


def body(
    spin_values,
    features,
    spin_embed,
    norm_gain,
    up_weight,
    down_weight,
    readout,
    local_energy,
    damping,
):
    samp_dev, length, model_width = features.shape
    hidden_dev = up_weight.shape[1]
    samp_size = lax.axis_size(SAMPLES)
    mp_size = lax.axis_size(MP)
    sample_count = samp_dev * samp_size
    rows_dev = model_width // samp_size
    share_rows = length // mp_size
    place = lax.axis_index(MP).astype(jnp.int32)
    readout_wide = readout.astype(jnp.float32)
    unit = jnp.maximum(jnp.max(jnp.abs(readout_wide)), 1e-30).reshape(1)
    feature_blocks = features.reshape(samp_dev, mp_size, share_rows, model_width)

    def partner(array, k):
        return lax.ppermute(array, MP, [(i, i ^ k) for i in range(mp_size)])

    with jax.named_scope("energy"):
        energy_row = jnp.zeros((1, sample_count), jnp.float32)
        first = 0
        for samples in CHUNKS:
            energy_row = lax.dynamic_update_slice(
                energy_row,
                local_energy[first : first + samples].reshape(1, samples),
                (0, first * samp_size + lax.axis_index(SAMPLES) * samples),
            )
            first += samples
        energy_row = jnp.where(place == 0, energy_row, 0.0)

    states = []
    first = 0
    for n, samples in enumerate(CHUNKS):
        with jax.named_scope("forward"):
            states.append(
                forward(
                    place.reshape(1),
                    spin_values,
                    feature_blocks,
                    spin_embed,
                    norm_gain,
                    up_weight,
                    down_weight,
                    first,
                    samples,
                    n > 0,
                )
            )
        first += samples
    coded_chunks = []
    for n, (normed, bend, *parts) in enumerate(states):
        if n > 0:
            own_inputs, _, *parts = parts
        with jax.named_scope("mixed_exchange"):
            if n == 0:
                mixed_parts = lax.all_to_all(parts[0], MP, 0, 0)
            else:
                mixed_other = parts[1].astype(jnp.float32)
                for k in range(3, mp_size, 2):
                    mixed_other = mixed_other + partner(parts[k], k - 1).astype(jnp.float32)
                mixed_other = partner(mixed_other.astype(jnp.bfloat16), 1)
                mixed_own = own_inputs + parts[0].astype(jnp.float32)
                for k in range(2, mp_size, 2):
                    mixed_own = mixed_own + partner(parts[k], k).astype(jnp.float32)
        with jax.named_scope("slope"):
            if n == 0:
                slope = own_slope(
                    place.reshape(1), mixed_parts, spin_values, feature_blocks, spin_embed, readout
                )
            else:
                outputs = mixed_own + mixed_other.astype(jnp.float32)
                slope = (readout_wide * jnp.tanh(outputs)).astype(jnp.bfloat16)
        with jax.named_scope("slope_share"):
            if n == 0:
                slopes = [lax.all_to_all(slope, MP, 0, 0)]
            else:
                other = partner(slope, 1)
                slopes = [slope, other]
                for k in range(2, mp_size, 2):
                    slopes += [partner(slope, k), partner(other, k)]
        with jax.named_scope("derivatives"):
            after = [state[3] for state in states[n + 1 : n + 2]]
            coded_chunks.append(
                derivative(1.0 / unit, normed, bend, down_weight, slopes, samp_size, after)
            )
    with jax.named_scope("derivative_exchange"):
        chunks = [lax.all_to_all(c, SAMPLES, 0, 0) for c in coded_chunks]
        chunks = [c.reshape(-1, rows_dev, hidden_dev) for c in chunks]
    with jax.named_scope("gram"):
        halves, wides = zip(*[rows_first(c) for c in chunks[:-1]])
        gram_part, last_wide = gram_matrix(energy_row, chunks[-1], halves)
        wides = wides + (last_wide,)
    with jax.named_scope("gram_sum"):
        near_size = lax.axis_size(NEAR)
        blocks = lax.all_to_all(
            gram_part.reshape(near_size, sample_count // near_size, sample_count), NEAR, 0, 0
        )
        blocks = share(jnp.sum(blocks, axis=0), FAR)
        shared = share(jnp.sum(blocks, axis=0), NEAR)
    with jax.named_scope("solve"):
        return solve(jnp.concatenate([damping, unit]), shared, wides, rows_dev)


def solution(mesh):
    samples, mp = mesh.devices.shape
    fine = jax.sharding.Mesh(
        mesh.devices.reshape(samples // 4, 2, 2, mp // 2, 2), SAMPLES + MP
    )
    in_specs = (
        P(SAMPLES, None),
        P(SAMPLES, None, None),
        P(),
        P(),
        P(None, MP),
        P(None, MP),
        P(),
        P(SAMPLES),
        P(),
    )
    out_specs = P(SAMPLES, MP)
    return jax.shard_map(body, mesh=fine, in_specs=in_specs, out_specs=out_specs, check_vma=False)
```

```python
import functools

import jax
import jax.numpy as jnp
from jax import lax
from jax.experimental import pallas as pl
from jax.experimental.pallas import tpu as pltpu
from jax.sharding import PartitionSpec as P

ITERS = 3
CHUNKS = (2, 2)
VMEM_LIMIT = 60 * 1024 * 1024
VMEM_SMALL = 32 * 1024 * 1024
SAMPLES = ("z", "x_lo", "core")
MP = ("y", "x_hi")
NEAR = ("z", "core")
FAR = ("x_lo", "y", "x_hi")


gelu_coef = 0.7978845608028654
cubic_coef = 0.044715


def encode(value):
    square = value * value
    return jnp.where(value < 0, -square * square, square * square).astype(jnp.bfloat16)


def decode(code):
    code = code.astype(jnp.float32)
    root = lax.rsqrt(lax.rsqrt(jnp.abs(code)))
    root = jnp.where(code == 0, 0.0, root)
    return jnp.where(code < 0, -root, root)


def share(array, axis):
    size = lax.axis_size(axis)
    return lax.all_to_all(jnp.broadcast_to(array, (size,) + array.shape), axis, 0, 0)


VMEM = pl.BlockSpec(memory_space=pltpu.VMEM)
SMEM = pl.BlockSpec(memory_space=pltpu.SMEM)


def forward_kernel(first, pairs, *refs):
    if pairs:
        order_ref, *refs = refs
        order = order_ref[0]
    spin_ref, feature_ref, embed_ref, gain_ref, up_ref, down_ref, normed_ref, bend_ref, *refs = refs
    blocks, rows, width = feature_ref.shape[1:]
    spin_row = spin_ref[pl.ds(first + pl.program_id(0), 1)].astype(jnp.float32)
    offset = lax.broadcasted_iota(jnp.int32, (rows, blocks * rows), 1) - lax.broadcasted_iota(
        jnp.int32, (rows, blocks * rows), 0
    )
    embed = embed_ref[...].astype(jnp.float32).reshape(1, width)
    gain = gain_ref[...].astype(jnp.float32).reshape(1, width)

    def block_inputs(block):
        spin_col = jnp.sum(jnp.where(offset == block * rows, spin_row, 0.0), axis=1, keepdims=True)
        return feature_ref[0, block].astype(jnp.float32) + spin_col * embed

    part_refs = refs
    if pairs:
        own_ref, mark_ref, *part_refs = refs
        own_ref[0] = block_inputs(order)
        mark_ref[...] = jnp.zeros_like(mark_ref)
    for k in range(blocks):
        inputs = block_inputs(jnp.bitwise_xor(order, k) if pairs else k)
        inv_scale = lax.rsqrt(jnp.mean(inputs * inputs, axis=1, keepdims=True) + 1e-05)
        normed_ref[0, k * rows : (k + 1) * rows] = (inputs * inv_scale * gain).astype(jnp.bfloat16)
    hidden_pre = jnp.dot(normed_ref[0], up_ref[...], preferred_element_type=jnp.float32)
    square = hidden_pre * hidden_pre
    inner_tanh = jnp.tanh(gelu_coef * (hidden_pre + cubic_coef * square * hidden_pre))
    activated = (0.5 * hidden_pre * (1.0 + inner_tanh)).astype(jnp.bfloat16)
    bend_ref[0] = 0.5 * (1.0 + inner_tanh) + 0.5 * hidden_pre * (
        1.0 - inner_tanh * inner_tanh
    ) * gelu_coef * (1.0 + 3.0 * cubic_coef * square)
    mixed = lax.dot_general(
        activated, down_ref[...], (((1,), (1,)), ((), ())), preferred_element_type=jnp.float32
    ).astype(jnp.bfloat16)
    for k in range(blocks):
        part = mixed[k * rows : (k + 1) * rows]
        per_ref = part_refs[0].shape[0]
        part_refs[k // per_ref][k % per_ref, 0] = part


def forward(order, spins, features, embed, gain, up, down, first, samples, pairs):
    _, blocks, rows, width = features.shape
    hidden = up.shape[1]
    tokens = blocks * rows
    whole = lambda array: pl.BlockSpec(array.shape, lambda s: (0,) * array.ndim)
    block = lambda *shape: pl.BlockSpec((1,) + shape, lambda s: (s,) + (0,) * len(shape))
    result = lambda dtype, *shape: jax.ShapeDtypeStruct((samples,) + shape, dtype)
    together = 1 if pairs else blocks
    part_specs = [pl.BlockSpec((together, 1, rows, width), lambda s: (0, s, 0, 0))] * (
        blocks // together
    )
    part_shapes = [jax.ShapeDtypeStruct((together, samples, rows, width), jnp.bfloat16)] * (
        blocks // together
    )
    if pairs:
        part_specs = [block(rows, width), pl.BlockSpec((8, 128), lambda s: (0, 0))] + part_specs
        part_shapes = [
            result(jnp.float32, rows, width),
            jax.ShapeDtypeStruct((8, 128), jnp.float32),
        ] + part_shapes
    return pl.pallas_call(
        functools.partial(forward_kernel, first, pairs),
        grid=(samples,),
        in_specs=[SMEM] * pairs
        + [
            whole(spins),
            pl.BlockSpec((1, blocks, rows, width), lambda s: (s + first, 0, 0, 0)),
            whole(embed),
            whole(gain),
            whole(up),
            whole(down),
        ],
        out_specs=[block(tokens, width), block(tokens, hidden)] + part_specs,
        out_shape=[
            result(jnp.bfloat16, tokens, width),
            result(jnp.float32, tokens, hidden),
        ]
        + part_shapes,
        compiler_params=pltpu.CompilerParams(vmem_limit_bytes=VMEM_LIMIT),
    )(*[order] * pairs, spins, features, embed, gain, up, down)


def slope_kernel(own_ref, part_ref, spin_ref, feature_ref, embed_ref, readout_ref, *refs):
    slope_ref = refs[-1]
    blocks, samples, rows, width = part_ref.shape
    own = own_ref[0]
    offset = lax.broadcasted_iota(jnp.int32, (rows, blocks * rows), 1) - lax.broadcasted_iota(
        jnp.int32, (rows, blocks * rows), 0
    )
    embed = embed_ref[...].astype(jnp.float32).reshape(1, width)
    readout = readout_ref[...].astype(jnp.float32).reshape(1, width)
    for s in range(samples):
        spin_row = spin_ref[s : s + 1].astype(jnp.float32)
        spin_col = jnp.sum(jnp.where(offset == own * rows, spin_row, 0.0), axis=1, keepdims=True)
        outputs = feature_ref[s, own].astype(jnp.float32) + spin_col * embed
        for k in range(blocks):
            outputs = outputs + part_ref[k, s].astype(jnp.float32)
        slope = (readout * jnp.tanh(outputs)).astype(jnp.bfloat16)
        slope_ref[0, s] = slope


def own_slope(own, parts, spins, features, embed, readout, after):
    whole = lambda array: pl.BlockSpec(array.shape, lambda s: (0,) * array.ndim)
    return pl.pallas_call(
        slope_kernel,
        grid=(1,),
        out_shape=pltpu.HBM((1,) + parts.shape[1:], parts.dtype),
        in_specs=[
            SMEM,
            whole(parts),
            whole(spins),
            pl.BlockSpec((parts.shape[1],) + features.shape[1:], lambda s: (0, 0, 0, 0)),
            whole(embed),
            whole(readout),
        ]
        + [pl.BlockSpec(memory_space=pl.ANY)] * len(after),
        out_specs=pl.BlockSpec((1,) + parts.shape[1:], lambda s: (0, 0, 0, 0)),
        compiler_params=pltpu.CompilerParams(vmem_limit_bytes=VMEM_SMALL),
    )(own, parts, spins, features, embed, readout, *after)


def derivative_kernel(order_ref, scale_ref, normed_ref, bend_ref, down_ref, *refs):
    *slope_refs, coded_ref, slope_ref = refs
    tokens, width = normed_ref.shape[1:]
    rows = slope_refs[0].shape[2]
    for k, received_ref in enumerate(slope_refs):
        start = pl.multiple_of(jnp.bitwise_xor(order_ref[0], k) * rows, rows)
        slope_ref[pl.ds(start, rows)] = received_ref[0, 0]
    slope = slope_ref[...]
    back_proj = jnp.dot(slope, down_ref[...], preferred_element_type=jnp.float32)
    pullback = (bend_ref[0] * back_proj).astype(jnp.bfloat16)
    deriv = lax.dot_general(
        normed_ref[0], pullback, (((0,), (0,)), ((), ())), preferred_element_type=jnp.float32
    )
    coded = encode(deriv * scale_ref[0])
    coded_ref[:, 0] = coded.reshape(coded_ref.shape[0], coded_ref.shape[2], coded_ref.shape[3])


def derivative(order, scale, normed, bend, down, slopes, parts, limit):
    samples, tokens, width = normed.shape
    hidden = down.shape[1]
    block = lambda *shape: pl.BlockSpec((1,) + shape, lambda s: (s,) + (0,) * len(shape))
    return pl.pallas_call(
        derivative_kernel,
        grid=(samples,),
        in_specs=[
            SMEM,
            SMEM,
            block(tokens, width),
            block(tokens, hidden),
            pl.BlockSpec(down.shape, lambda s: (0, 0)),
        ]
        + [
            pl.BlockSpec((a.shape[0], 1) + a.shape[2:], lambda s: (0, s, 0, 0))
            for a in slopes
        ],
        out_specs=pl.BlockSpec((parts, 1, width // parts, hidden), lambda s: (0, s, 0, 0)),
        out_shape=pltpu.HBM((parts, samples, width // parts, hidden), jnp.bfloat16),
        scratch_shapes=[pltpu.VMEM((tokens, width), jnp.bfloat16)],
        compiler_params=pltpu.CompilerParams(vmem_limit_bytes=limit),
    )(order, scale, normed, bend, down, *slopes)


LANES = 128


STEP = 16


def widen(code_ref, wide_ref, apart_ref):
    count, rows, _ = code_ref.shape
    for n in range(count):
        values = decode(code_ref[n])
        for f in range(wide_ref.shape[1]):
            group = values[:, f * LANES : (f + 1) * LANES]
            wide_ref[0, f, n * rows : (n + 1) * rows] = group
            apart_ref[f, n * (rows + 1) : n * (rows + 1) + rows] = group


def row_of_all(apart_ref, row, count, rows):
    groups = [apart_ref[f, pl.ds(row, count, stride=rows + 1)] for f in range(apart_ref.shape[0])]
    return jnp.concatenate(groups, axis=1).astype(jnp.bfloat16)


def apart_scratch(count, width):
    return pltpu.VMEM((width // LANES, -(-count * (STEP + 1) // 8) * 8, LANES), jnp.float32)


def wide_out(count, rows, width):
    return (
        pl.BlockSpec((1, width // LANES, count * STEP, LANES), lambda r: (r, 0, 0, 0)),
        pltpu.HBM((rows // STEP, width // LANES, count * STEP, LANES), jnp.float32),
    )


def rows_first_kernel(code_ref, half_ref, wide_ref, apart_ref):
    count, rows, _ = code_ref.shape
    widen(code_ref, wide_ref, apart_ref)
    for r in range(rows):
        half_ref[r] = row_of_all(apart_ref, r, count, rows)


def rows_first(code):
    count, rows, width = code.shape
    wide_spec, wide_shape = wide_out(count, rows, width)
    return pl.pallas_call(
        rows_first_kernel,
        grid=(rows // STEP,),
        in_specs=[pl.BlockSpec((count, STEP, width), lambda r: (0, r, 0))],
        out_specs=[pl.BlockSpec((STEP, count, width), lambda r: (r, 0, 0)), wide_spec],
        out_shape=[jax.ShapeDtypeStruct((rows, count, width), jnp.bfloat16), wide_shape],
        scratch_shapes=[apart_scratch(count, width)],
        compiler_params=pltpu.CompilerParams(vmem_limit_bytes=VMEM_SMALL),
    )(code)


def gram_kernel(energy_ref, code_ref, *refs):
    half_refs, gram_ref, wide_ref, apart_ref = refs[:-3], *refs[-3:]
    count, rows, _ = code_ref.shape
    widen(code_ref, wide_ref, apart_ref)
    gram = jnp.zeros(gram_ref.shape, jnp.float32)
    for r in range(rows):
        half = jnp.concatenate(
            [h[r] for h in half_refs] + [row_of_all(apart_ref, r, count, rows)], axis=0
        )
        gram += lax.dot_general(half, half, (((1,), (1,)), ((), ())), preferred_element_type=jnp.float32)

    @pl.when(pl.program_id(0) == 0)
    def _():
        gram_ref[...] = gram

    @pl.when(pl.program_id(0) > 0)
    def _():
        gram_ref[...] += gram

    @pl.when(pl.program_id(0) == pl.num_programs(0) - 1)
    def _():
        total = gram_ref[...]
        size = total.shape[0]
        row = lax.broadcasted_iota(jnp.int32, total.shape, 0)
        col = lax.broadcasted_iota(jnp.int32, total.shape, 1)
        energy = energy_ref[...]
        total = jnp.where((row == size - 1) & (col < size - 1), energy, total)
        last_energy = jnp.sum(jnp.where(col[:1] == size - 1, energy, 0.0), axis=1, keepdims=True)
        gram_ref[...] = jnp.where((row == size - 2) & (col == 0), last_energy, total)


def gram_matrix(energy, code, halves):
    count, rows, width = code.shape
    size = energy.shape[1]
    wide_spec, wide_shape = wide_out(count, rows, width)
    return pl.pallas_call(
        gram_kernel,
        grid=(rows // STEP,),
        in_specs=[
            pl.BlockSpec(energy.shape, lambda f: (0, 0)),
            pl.BlockSpec((count, STEP, width), lambda r: (0, r, 0)),
        ]
        + [pl.BlockSpec((STEP,) + h.shape[1:], lambda r: (r, 0, 0)) for h in halves],
        out_specs=[pl.BlockSpec((size, size), lambda f: (0, 0)), wide_spec],
        out_shape=[jax.ShapeDtypeStruct((size, size), jnp.float32), wide_shape],
        scratch_shapes=[apart_scratch(count, width)],
        compiler_params=pltpu.CompilerParams(vmem_limit_bytes=VMEM_LIMIT),
    )(energy, code, *halves)


def solve_kernel(scalar_ref, shared_ref, *refs):
    chunk_count = (len(refs) - 4) // 2
    far_refs, out_ref, gram_ref, spread_ref = refs[:chunk_count], *refs[chunk_count : chunk_count + 3]
    chunk_refs, sems = refs[chunk_count + 3 : -1], refs[-1]
    copies = [
        pltpu.make_async_copy(far, near, sems.at[n])
        for n, (far, near) in enumerate(zip(far_refs, chunk_refs))
    ]
    for copy in copies:
        copy.start()
    count = gram_ref.shape[0]
    gram_rows = shared_ref.shape[1]
    damping, unit = scalar_ref[0], scalar_ref[1]
    for device in range(shared_ref.shape[0]):
        gram_ref[device * gram_rows : (device + 1) * gram_rows] = shared_ref[device]
    row = lax.broadcasted_iota(jnp.int32, (count, count), 0)
    col = lax.broadcasted_iota(jnp.int32, (count, count), 1)
    gram = gram_ref[...]
    energy_row = jnp.where(
        col[:1] == count - 1, gram_ref[count - 2 : count - 1, 0:1], gram_ref[count - 1 : count]
    )
    energy_col = jnp.sum(jnp.where(row == col, energy_row, 0.0), axis=1, keepdims=True)
    gram = jnp.where(row <= col, gram, gram.T) * (unit * unit)
    gram = gram - jnp.sum(gram, axis=1, keepdims=True) / count
    gram = gram - jnp.sum(gram, axis=0, keepdims=True) / count

    def center(row, col):
        return (
            (row - jnp.sum(row, axis=1, keepdims=True) / count) / count,
            (col - jnp.sum(col, axis=0, keepdims=True) / count) / count,
        )

    def apply(row, col):
        return jnp.sum(gram * col, axis=0, keepdims=True), jnp.sum(gram * row, axis=1, keepdims=True)

    def inner(row, other):
        return jnp.sum(row * other, axis=1, keepdims=True)

    residual = center(energy_row, energy_col)
    direction = residual
    coef = jnp.zeros_like(residual[1])
    norm_now = inner(residual[0], apply(*residual)[0])
    for iteration in range(ITERS):
        values = apply(*direction)
        weights = center(*values)
        image = tuple(w + damping * d for w, d in zip(weights, direction))
        step_size = norm_now / inner(values[0], image[0])
        coef = coef + step_size * direction[1]
        if iteration < ITERS - 1:
            residual = tuple(r - step_size * i for r, i in zip(residual, image))
            norm_next = inner(residual[0], apply(*residual)[0])
            ratio = norm_next / norm_now
            direction = tuple(r + ratio * d for r, d in zip(residual, direction))
            norm_now = norm_next
    spread_ref[...] = jnp.broadcast_to(coef * unit, spread_ref.shape)
    lanes = spread_ref.shape[1]
    first = 0
    for n, chunk_ref in enumerate(chunk_refs):
        copies[n].wait()
        steps, groups, depth, _ = chunk_ref.shape
        for r in range(steps):
            here = slice(r * STEP, (r + 1) * STEP)

            def add(s, total):
                start = pl.multiple_of(s * STEP, STEP)
                spread = spread_ref[pl.ds(first + s, 1)]
                return tuple(t + spread * chunk_ref[r, f, pl.ds(start, STEP)] for f, t in enumerate(total))

            total = tuple(
                out_ref[here, f * lanes : (f + 1) * lanes] if n else jnp.zeros((STEP, lanes), jnp.float32)
                for f in range(groups)
            )
            total = lax.fori_loop(0, depth // STEP, add, total, unroll=8)
            for f, t in enumerate(total):
                out_ref[here, f * lanes : (f + 1) * lanes] = t
        first += depth // STEP


def solve(scalars, shared, chunks, rows):
    count = shared.shape[2]
    return pl.pallas_call(
        solve_kernel,
        out_shape=jax.ShapeDtypeStruct((rows, chunks[0].shape[1] * chunks[0].shape[3]), jnp.float32),
        in_specs=[SMEM, VMEM] + [pl.BlockSpec(memory_space=pltpu.HBM)] * len(chunks),
        out_specs=VMEM,
        scratch_shapes=[
            pltpu.VMEM((count, count), jnp.float32),
            pltpu.VMEM((count, LANES), jnp.float32),
        ]
        + [pltpu.VMEM(c.shape, c.dtype) for c in chunks]
        + [pltpu.SemaphoreType.DMA((len(chunks),))],
        compiler_params=pltpu.CompilerParams(vmem_limit_bytes=VMEM_LIMIT),
    )(scalars, shared, *chunks)


def body(
    spin_values,
    features,
    spin_embed,
    norm_gain,
    up_weight,
    down_weight,
    readout,
    local_energy,
    damping,
):
    samp_dev, length, model_width = features.shape
    hidden_dev = up_weight.shape[1]
    samp_size = lax.axis_size(SAMPLES)
    mp_size = lax.axis_size(MP)
    sample_count = samp_dev * samp_size
    rows_dev = model_width // samp_size
    share_rows = length // mp_size
    place = lax.axis_index(MP).astype(jnp.int32)
    readout_wide = readout.astype(jnp.float32)
    unit = jnp.maximum(jnp.max(jnp.abs(readout_wide)), 1e-30).reshape(1)
    feature_blocks = features.reshape(samp_dev, mp_size, share_rows, model_width)

    def partner(array, k):
        return lax.ppermute(array, MP, [(i, i ^ k) for i in range(mp_size)])

    with jax.named_scope("energy"):
        energy_row = jnp.zeros((1, sample_count), jnp.float32)
        first = 0
        for samples in CHUNKS:
            energy_row = lax.dynamic_update_slice(
                energy_row,
                local_energy[first : first + samples].reshape(1, samples),
                (0, first * samp_size + lax.axis_index(SAMPLES) * samples),
            )
            first += samples
        energy_row = jnp.where(place == 0, energy_row, 0.0)

    states = []
    first = 0
    for n, samples in enumerate(CHUNKS):
        with jax.named_scope("forward"):
            states.append(
                forward(
                    place.reshape(1),
                    spin_values,
                    feature_blocks,
                    spin_embed,
                    norm_gain,
                    up_weight,
                    down_weight,
                    first,
                    samples,
                    n > 0,
                )
            )
        first += samples
    coded_chunks = []
    for n, (normed, bend, *parts) in enumerate(states):
        if n > 0:
            own_inputs, _, *parts = parts
            *parts, coded_chunks[-1] = lax.optimization_barrier((*parts, coded_chunks[-1]))
        with jax.named_scope("mixed_exchange"):
            if n == 0:
                mixed_parts = lax.all_to_all(parts[0], MP, 0, 0)
            else:
                mixed_other = parts[1].astype(jnp.float32)
                for k in range(3, mp_size, 2):
                    mixed_other = mixed_other + partner(parts[k], k - 1).astype(jnp.float32)
                mixed_other = partner(mixed_other.astype(jnp.bfloat16), 1)
                mixed_own = own_inputs + parts[0].astype(jnp.float32)
                for k in range(2, mp_size, 2):
                    mixed_own = mixed_own + partner(parts[k], k).astype(jnp.float32)
        with jax.named_scope("slope"):
            if n == 0:
                slope = own_slope(
                    place.reshape(1),
                    mixed_parts,
                    spin_values,
                    feature_blocks,
                    spin_embed,
                    readout,
                    [state[3] for state in states[1:2]],
                )
            else:
                outputs = mixed_own + mixed_other.astype(jnp.float32)
                slope = (readout_wide * jnp.tanh(outputs)).astype(jnp.bfloat16)
        with jax.named_scope("slope_share"):
            other = partner(slope, 1)
            slopes = [slope, other]
            for k in range(2, mp_size, 2):
                slopes += [partner(slope, k), partner(other, k)]
        with jax.named_scope("derivatives"):
            order = jnp.zeros((1,), jnp.int32) if n else place.reshape(1)
            coded_chunks.append(
                derivative(
                    order,
                    1.0 / unit,
                    normed,
                    bend,
                    down_weight,
                    slopes,
                    samp_size,
                    VMEM_SMALL if n else VMEM_LIMIT,
                )
            )
    with jax.named_scope("derivative_exchange"):
        chunks = [lax.all_to_all(c, SAMPLES, 0, 0) for c in coded_chunks]
        chunks = [c.reshape(-1, rows_dev, hidden_dev) for c in chunks]
    with jax.named_scope("gram"):
        halves, wides = zip(*[rows_first(c) for c in chunks[:-1]])
        gram_part, last_wide = gram_matrix(energy_row, chunks[-1], halves)
        wides = wides + (last_wide,)
    with jax.named_scope("gram_sum"):
        near_size = lax.axis_size(NEAR)
        blocks = lax.all_to_all(
            gram_part.reshape(near_size, sample_count // near_size, sample_count), NEAR, 0, 0
        )
        blocks = share(jnp.sum(blocks, axis=0), FAR)
        shared = share(jnp.sum(blocks, axis=0), NEAR)
    with jax.named_scope("solve"):
        return solve(jnp.concatenate([damping, unit]), shared, wides, rows_dev)


def solution(mesh):
    samples, mp = mesh.devices.shape
    fine = jax.sharding.Mesh(
        mesh.devices.reshape(samples // 4, 2, 2, mp // 2, 2), SAMPLES + MP
    )
    in_specs = (
        P(SAMPLES, None),
        P(SAMPLES, None, None),
        P(),
        P(),
        P(None, MP),
        P(None, MP),
        P(),
        P(SAMPLES),
        P(),
    )
    out_specs = P(SAMPLES, MP)
    return jax.shard_map(body, mesh=fine, in_specs=in_specs, out_specs=out_specs, check_vma=False)
```

```python
import functools

import jax
import jax.numpy as jnp
from jax import lax
from jax.experimental import pallas as pl
from jax.experimental.pallas import tpu as pltpu
from jax.sharding import PartitionSpec as P

ITERS = 3
CHUNKS = (2, 2)
VMEM_LIMIT = 60 * 1024 * 1024
VMEM_SMALL = 32 * 1024 * 1024
SAMPLES = ("z", "x_lo", "core")
MP = ("y", "x_hi")
NEAR = ("z", "core")
FAR = ("x_lo", "y", "x_hi")


gelu_coef = 0.7978845608028654
cubic_coef = 0.044715


def encode(value):
    square = value * value
    return jnp.where(value < 0, -square * square, square * square).astype(jnp.bfloat16)


def decode(code):
    code = code.astype(jnp.float32)
    root = lax.rsqrt(lax.rsqrt(jnp.abs(code)))
    root = jnp.where(code == 0, 0.0, root)
    return jnp.where(code < 0, -root, root)


def share(array, axis):
    size = lax.axis_size(axis)
    return lax.all_to_all(jnp.broadcast_to(array, (size,) + array.shape), axis, 0, 0)


VMEM = pl.BlockSpec(memory_space=pltpu.VMEM)
SMEM = pl.BlockSpec(memory_space=pltpu.SMEM)


def forward_kernel(first, pairs, *refs):
    if pairs:
        order_ref, *refs = refs
        order = order_ref[0]
    spin_ref, feature_ref, embed_ref, gain_ref, up_ref, down_ref, normed_ref, bend_ref, *refs = refs
    blocks, rows, width = feature_ref.shape[1:]
    spin_row = spin_ref[pl.ds(first + pl.program_id(0), 1)].astype(jnp.float32)
    offset = lax.broadcasted_iota(jnp.int32, (rows, blocks * rows), 1) - lax.broadcasted_iota(
        jnp.int32, (rows, blocks * rows), 0
    )
    embed = embed_ref[...].astype(jnp.float32).reshape(1, width)
    gain = gain_ref[...].astype(jnp.float32).reshape(1, width)

    def block_inputs(block):
        spin_col = jnp.sum(jnp.where(offset == block * rows, spin_row, 0.0), axis=1, keepdims=True)
        return feature_ref[0, block].astype(jnp.float32) + spin_col * embed

    part_refs = refs
    if pairs:
        own_ref, mark_ref, *part_refs = refs
        own_ref[0] = block_inputs(order)
        mark_ref[...] = jnp.zeros_like(mark_ref)
    for k in range(blocks):
        inputs = block_inputs(jnp.bitwise_xor(order, k) if pairs else k)
        inv_scale = lax.rsqrt(jnp.mean(inputs * inputs, axis=1, keepdims=True) + 1e-05)
        normed_ref[0, k * rows : (k + 1) * rows] = (inputs * inv_scale * gain).astype(jnp.bfloat16)
    hidden_pre = jnp.dot(normed_ref[0], up_ref[...], preferred_element_type=jnp.float32)
    square = hidden_pre * hidden_pre
    inner_tanh = jnp.tanh(gelu_coef * (hidden_pre + cubic_coef * square * hidden_pre))
    activated = (0.5 * hidden_pre * (1.0 + inner_tanh)).astype(jnp.bfloat16)
    bend_ref[0] = 0.5 * (1.0 + inner_tanh) + 0.5 * hidden_pre * (
        1.0 - inner_tanh * inner_tanh
    ) * gelu_coef * (1.0 + 3.0 * cubic_coef * square)
    mixed = lax.dot_general(
        activated, down_ref[...], (((1,), (1,)), ((), ())), preferred_element_type=jnp.float32
    ).astype(jnp.bfloat16)
    for k in range(blocks):
        part = mixed[k * rows : (k + 1) * rows]
        per_ref = part_refs[0].shape[0]
        part_refs[k // per_ref][k % per_ref, 0] = part


def forward(order, spins, features, embed, gain, up, down, first, samples, pairs):
    _, blocks, rows, width = features.shape
    hidden = up.shape[1]
    tokens = blocks * rows
    whole = lambda array: pl.BlockSpec(array.shape, lambda s: (0,) * array.ndim)
    block = lambda *shape: pl.BlockSpec((1,) + shape, lambda s: (s,) + (0,) * len(shape))
    result = lambda dtype, *shape: jax.ShapeDtypeStruct((samples,) + shape, dtype)
    together = 1 if pairs else blocks
    part_specs = [pl.BlockSpec((together, 1, rows, width), lambda s: (0, s, 0, 0))] * (
        blocks // together
    )
    part_shapes = [jax.ShapeDtypeStruct((together, samples, rows, width), jnp.bfloat16)] * (
        blocks // together
    )
    if pairs:
        part_specs = [block(rows, width), pl.BlockSpec((8, 128), lambda s: (0, 0))] + part_specs
        part_shapes = [
            result(jnp.float32, rows, width),
            jax.ShapeDtypeStruct((8, 128), jnp.float32),
        ] + part_shapes
    return pl.pallas_call(
        functools.partial(forward_kernel, first, pairs),
        grid=(samples,),
        in_specs=[SMEM] * pairs
        + [
            whole(spins),
            pl.BlockSpec((1, blocks, rows, width), lambda s: (s + first, 0, 0, 0)),
            whole(embed),
            whole(gain),
            whole(up),
            whole(down),
        ],
        out_specs=[block(tokens, width), block(tokens, hidden)] + part_specs,
        out_shape=[
            result(jnp.bfloat16, tokens, width),
            result(jnp.float32, tokens, hidden),
        ]
        + part_shapes,
        compiler_params=pltpu.CompilerParams(vmem_limit_bytes=VMEM_LIMIT),
    )(*[order] * pairs, spins, features, embed, gain, up, down)


def slope_kernel(own_ref, part_ref, spin_ref, feature_ref, embed_ref, readout_ref, *refs):
    slope_ref = refs[-1]
    blocks, samples, rows, width = part_ref.shape
    own = own_ref[0]
    offset = lax.broadcasted_iota(jnp.int32, (rows, blocks * rows), 1) - lax.broadcasted_iota(
        jnp.int32, (rows, blocks * rows), 0
    )
    embed = embed_ref[...].astype(jnp.float32).reshape(1, width)
    readout = readout_ref[...].astype(jnp.float32).reshape(1, width)
    for s in range(samples):
        spin_row = spin_ref[s : s + 1].astype(jnp.float32)
        spin_col = jnp.sum(jnp.where(offset == own * rows, spin_row, 0.0), axis=1, keepdims=True)
        outputs = feature_ref[s, own].astype(jnp.float32) + spin_col * embed
        for k in range(blocks):
            outputs = outputs + part_ref[k, s].astype(jnp.float32)
        slope = (readout * jnp.tanh(outputs)).astype(jnp.bfloat16)
        slope_ref[0, s] = slope


def own_slope(own, parts, spins, features, embed, readout, after):
    whole = lambda array: pl.BlockSpec(array.shape, lambda s: (0,) * array.ndim)
    return pl.pallas_call(
        slope_kernel,
        grid=(1,),
        out_shape=pltpu.HBM((1,) + parts.shape[1:], parts.dtype),
        in_specs=[
            SMEM,
            whole(parts),
            whole(spins),
            pl.BlockSpec((parts.shape[1],) + features.shape[1:], lambda s: (0, 0, 0, 0)),
            whole(embed),
            whole(readout),
        ]
        + [pl.BlockSpec(memory_space=pl.ANY)] * len(after),
        out_specs=pl.BlockSpec((1,) + parts.shape[1:], lambda s: (0, 0, 0, 0)),
        compiler_params=pltpu.CompilerParams(vmem_limit_bytes=VMEM_SMALL),
    )(own, parts, spins, features, embed, readout, *after)


def derivative_kernel(order_ref, scale_ref, normed_ref, bend_ref, down_ref, *refs):
    *slope_refs, coded_ref, slope_ref = refs
    tokens, width = normed_ref.shape[1:]
    rows = slope_refs[0].shape[2]
    for k, received_ref in enumerate(slope_refs):
        start = pl.multiple_of(jnp.bitwise_xor(order_ref[0], k) * rows, rows)
        slope_ref[pl.ds(start, rows)] = received_ref[0, 0]
    slope = slope_ref[...]
    back_proj = jnp.dot(slope, down_ref[...], preferred_element_type=jnp.float32)
    pullback = (bend_ref[0] * back_proj).astype(jnp.bfloat16)
    deriv = lax.dot_general(
        normed_ref[0], pullback, (((0,), (0,)), ((), ())), preferred_element_type=jnp.float32
    )
    coded = encode(deriv * scale_ref[0])
    coded_ref[:, 0] = coded.reshape(coded_ref.shape[0], coded_ref.shape[2], coded_ref.shape[3])


def derivative(order, scale, normed, bend, down, slopes, parts, limit):
    samples, tokens, width = normed.shape
    hidden = down.shape[1]
    block = lambda *shape: pl.BlockSpec((1,) + shape, lambda s: (s,) + (0,) * len(shape))
    return pl.pallas_call(
        derivative_kernel,
        grid=(samples,),
        in_specs=[
            SMEM,
            SMEM,
            block(tokens, width),
            block(tokens, hidden),
            pl.BlockSpec(down.shape, lambda s: (0, 0)),
        ]
        + [
            pl.BlockSpec((a.shape[0], 1) + a.shape[2:], lambda s: (0, s, 0, 0))
            for a in slopes
        ],
        out_specs=pl.BlockSpec((parts, 1, width // parts, hidden), lambda s: (0, s, 0, 0)),
        out_shape=pltpu.HBM((parts, samples, width // parts, hidden), jnp.bfloat16),
        scratch_shapes=[pltpu.VMEM((tokens, width), jnp.bfloat16)],
        compiler_params=pltpu.CompilerParams(vmem_limit_bytes=limit),
    )(order, scale, normed, bend, down, *slopes)


LANES = 128


STEP = 16


def widen(code_ref, wide_ref, apart_ref):
    count, rows, _ = code_ref.shape
    for n in range(count):
        values = decode(code_ref[n])
        for f in range(wide_ref.shape[1]):
            group = values[:, f * LANES : (f + 1) * LANES]
            wide_ref[0, f, n * rows : (n + 1) * rows] = group
            apart_ref[f, n * (rows + 1) : n * (rows + 1) + rows] = group


def row_of_all(apart_ref, row, count, rows):
    groups = [apart_ref[f, pl.ds(row, count, stride=rows + 1)] for f in range(apart_ref.shape[0])]
    return jnp.concatenate(groups, axis=1).astype(jnp.bfloat16)


def apart_scratch(count, width):
    return pltpu.VMEM((width // LANES, -(-count * (STEP + 1) // 8) * 8, LANES), jnp.float32)


def wide_out(count, rows, width):
    return (
        pl.BlockSpec((1, width // LANES, count * STEP, LANES), lambda r: (r, 0, 0, 0)),
        pltpu.HBM((rows // STEP, width // LANES, count * STEP, LANES), jnp.float32),
    )


def rows_first_kernel(code_ref, half_ref, wide_ref, apart_ref):
    count, rows, _ = code_ref.shape
    widen(code_ref, wide_ref, apart_ref)
    for r in range(rows):
        half_ref[r] = row_of_all(apart_ref, r, count, rows)


def rows_first(code):
    count, rows, width = code.shape
    wide_spec, wide_shape = wide_out(count, rows, width)
    return pl.pallas_call(
        rows_first_kernel,
        grid=(rows // STEP,),
        in_specs=[pl.BlockSpec((count, STEP, width), lambda r: (0, r, 0))],
        out_specs=[pl.BlockSpec((STEP, count, width), lambda r: (r, 0, 0)), wide_spec],
        out_shape=[jax.ShapeDtypeStruct((rows, count, width), jnp.bfloat16), wide_shape],
        scratch_shapes=[apart_scratch(count, width)],
        compiler_params=pltpu.CompilerParams(vmem_limit_bytes=VMEM_SMALL),
    )(code)


def gram_kernel(energy_ref, code_ref, *refs):
    half_refs, gram_ref, wide_ref, apart_ref = refs[:-3], *refs[-3:]
    count, rows, _ = code_ref.shape
    widen(code_ref, wide_ref, apart_ref)
    gram = jnp.zeros(gram_ref.shape, jnp.float32)
    for r in range(rows):
        half = jnp.concatenate(
            [h[r] for h in half_refs] + [row_of_all(apart_ref, r, count, rows)], axis=0
        )
        gram += lax.dot_general(half, half, (((1,), (1,)), ((), ())), preferred_element_type=jnp.float32)

    @pl.when(pl.program_id(0) == 0)
    def _():
        gram_ref[...] = gram

    @pl.when(pl.program_id(0) > 0)
    def _():
        gram_ref[...] += gram

    @pl.when(pl.program_id(0) == pl.num_programs(0) - 1)
    def _():
        total = gram_ref[...]
        size = total.shape[0]
        row = lax.broadcasted_iota(jnp.int32, total.shape, 0)
        col = lax.broadcasted_iota(jnp.int32, total.shape, 1)
        energy = energy_ref[...]
        total = jnp.where((row == size - 1) & (col < size - 1), energy, total)
        last_energy = jnp.sum(jnp.where(col[:1] == size - 1, energy, 0.0), axis=1, keepdims=True)
        gram_ref[...] = jnp.where((row == size - 2) & (col == 0), last_energy, total)


def gram_matrix(energy, code, halves):
    count, rows, width = code.shape
    size = energy.shape[1]
    wide_spec, wide_shape = wide_out(count, rows, width)
    return pl.pallas_call(
        gram_kernel,
        grid=(rows // STEP,),
        in_specs=[
            pl.BlockSpec(energy.shape, lambda f: (0, 0)),
            pl.BlockSpec((count, STEP, width), lambda r: (0, r, 0)),
        ]
        + [pl.BlockSpec((STEP,) + h.shape[1:], lambda r: (r, 0, 0)) for h in halves],
        out_specs=[pl.BlockSpec((size, size), lambda f: (0, 0)), wide_spec],
        out_shape=[jax.ShapeDtypeStruct((size, size), jnp.float32), wide_shape],
        scratch_shapes=[apart_scratch(count, width)],
        compiler_params=pltpu.CompilerParams(vmem_limit_bytes=VMEM_LIMIT),
    )(energy, code, *halves)


def solve_kernel(scalar_ref, shared_ref, *refs):
    chunk_count = (len(refs) - 4) // 2
    far_refs, out_ref, gram_ref, spread_ref = refs[:chunk_count], *refs[chunk_count : chunk_count + 3]
    chunk_refs, sems = refs[chunk_count + 3 : -1], refs[-1]
    copies = {
        (n, r, f): pltpu.make_async_copy(far.at[r, f], near.at[r, f], sems.at[n, r, f])
        for n, (far, near) in enumerate(zip(far_refs, chunk_refs))
        for r in range(near.shape[0])
        for f in range(near.shape[1])
    }
    for copy in copies.values():
        copy.start()
    count = gram_ref.shape[0]
    gram_rows = shared_ref.shape[1]
    damping, unit = scalar_ref[0], scalar_ref[1]
    for device in range(shared_ref.shape[0]):
        gram_ref[device * gram_rows : (device + 1) * gram_rows] = shared_ref[device]
    row = lax.broadcasted_iota(jnp.int32, (count, count), 0)
    col = lax.broadcasted_iota(jnp.int32, (count, count), 1)
    gram = gram_ref[...]
    energy_row = jnp.where(
        col[:1] == count - 1, gram_ref[count - 2 : count - 1, 0:1], gram_ref[count - 1 : count]
    )
    energy_col = jnp.sum(jnp.where(row == col, energy_row, 0.0), axis=1, keepdims=True)
    gram = jnp.where(row <= col, gram, gram.T) * (unit * unit)
    gram = gram - jnp.sum(gram, axis=1, keepdims=True) / count
    gram = gram - jnp.sum(gram, axis=0, keepdims=True) / count

    def center(row, col):
        return (
            (row - jnp.sum(row, axis=1, keepdims=True) / count) / count,
            (col - jnp.sum(col, axis=0, keepdims=True) / count) / count,
        )

    def apply(row, col):
        return jnp.sum(gram * col, axis=0, keepdims=True), jnp.sum(gram * row, axis=1, keepdims=True)

    def inner(row, other):
        return jnp.sum(row * other, axis=1, keepdims=True)

    residual = center(energy_row, energy_col)
    direction = residual
    coef = jnp.zeros_like(residual[1])
    norm_now = inner(residual[0], apply(*residual)[0])
    for iteration in range(ITERS):
        values = apply(*direction)
        weights = center(*values)
        image = tuple(w + damping * d for w, d in zip(weights, direction))
        step_size = norm_now / inner(values[0], image[0])
        coef = coef + step_size * direction[1]
        if iteration < ITERS - 1:
            residual = tuple(r - step_size * i for r, i in zip(residual, image))
            norm_next = inner(residual[0], apply(*residual)[0])
            ratio = norm_next / norm_now
            direction = tuple(r + ratio * d for r, d in zip(residual, direction))
            norm_now = norm_next
    spread_ref[...] = jnp.broadcast_to(coef * unit, spread_ref.shape)
    lanes = spread_ref.shape[1]
    first = 0
    for n, chunk_ref in enumerate(chunk_refs):
        steps, groups, depth, _ = chunk_ref.shape
        for r in range(steps):
            for f in range(groups):
                copies[n, r, f].wait()
            here = slice(r * STEP, (r + 1) * STEP)

            def add(s, total):
                start = pl.multiple_of(s * STEP, STEP)
                spread = spread_ref[pl.ds(first + s, 1)]
                return tuple(t + spread * chunk_ref[r, f, pl.ds(start, STEP)] for f, t in enumerate(total))

            total = tuple(
                out_ref[here, f * lanes : (f + 1) * lanes] if n else jnp.zeros((STEP, lanes), jnp.float32)
                for f in range(groups)
            )
            total = lax.fori_loop(0, depth // STEP, add, total, unroll=8)
            for f, t in enumerate(total):
                out_ref[here, f * lanes : (f + 1) * lanes] = t
        first += depth // STEP


def solve(scalars, shared, chunks, rows):
    count = shared.shape[2]
    return pl.pallas_call(
        solve_kernel,
        out_shape=jax.ShapeDtypeStruct((rows, chunks[0].shape[1] * chunks[0].shape[3]), jnp.float32),
        in_specs=[SMEM, VMEM] + [pl.BlockSpec(memory_space=pltpu.HBM)] * len(chunks),
        out_specs=VMEM,
        scratch_shapes=[
            pltpu.VMEM((count, count), jnp.float32),
            pltpu.VMEM((count, LANES), jnp.float32),
        ]
        + [pltpu.VMEM(c.shape, c.dtype) for c in chunks]
        + [pltpu.SemaphoreType.DMA((len(chunks),) + chunks[0].shape[:2])],
        compiler_params=pltpu.CompilerParams(vmem_limit_bytes=VMEM_LIMIT),
    )(scalars, shared, *chunks)


def body(
    spin_values,
    features,
    spin_embed,
    norm_gain,
    up_weight,
    down_weight,
    readout,
    local_energy,
    damping,
):
    samp_dev, length, model_width = features.shape
    hidden_dev = up_weight.shape[1]
    samp_size = lax.axis_size(SAMPLES)
    mp_size = lax.axis_size(MP)
    sample_count = samp_dev * samp_size
    rows_dev = model_width // samp_size
    share_rows = length // mp_size
    place = lax.axis_index(MP).astype(jnp.int32)
    readout_wide = readout.astype(jnp.float32)
    unit = jnp.maximum(jnp.max(jnp.abs(readout_wide)), 1e-30).reshape(1)
    feature_blocks = features.reshape(samp_dev, mp_size, share_rows, model_width)

    def partner(array, k):
        return lax.ppermute(array, MP, [(i, i ^ k) for i in range(mp_size)])

    with jax.named_scope("energy"):
        energy_row = jnp.zeros((1, sample_count), jnp.float32)
        first = 0
        for samples in CHUNKS:
            energy_row = lax.dynamic_update_slice(
                energy_row,
                local_energy[first : first + samples].reshape(1, samples),
                (0, first * samp_size + lax.axis_index(SAMPLES) * samples),
            )
            first += samples
        energy_row = jnp.where(place == 0, energy_row, 0.0)

    states = []
    first = 0
    for n, samples in enumerate(CHUNKS):
        with jax.named_scope("forward"):
            states.append(
                forward(
                    place.reshape(1),
                    spin_values,
                    feature_blocks,
                    spin_embed,
                    norm_gain,
                    up_weight,
                    down_weight,
                    first,
                    samples,
                    n > 0,
                )
            )
        first += samples
    coded_chunks = []
    for n, (normed, bend, *parts) in enumerate(states):
        if n > 0:
            own_inputs, _, *parts = parts
            *parts, coded_chunks[-1] = lax.optimization_barrier((*parts, coded_chunks[-1]))
        with jax.named_scope("mixed_exchange"):
            if n == 0:
                mixed_parts = lax.all_to_all(parts[0], MP, 0, 0)
            else:
                mixed_other = parts[1].astype(jnp.float32)
                for k in range(3, mp_size, 2):
                    mixed_other = mixed_other + partner(parts[k], k - 1).astype(jnp.float32)
                mixed_other = partner(mixed_other.astype(jnp.bfloat16), 1)
                mixed_own = own_inputs + parts[0].astype(jnp.float32)
                for k in range(2, mp_size, 2):
                    mixed_own = mixed_own + partner(parts[k], k).astype(jnp.float32)
        with jax.named_scope("slope"):
            if n == 0:
                slope = own_slope(
                    place.reshape(1),
                    mixed_parts,
                    spin_values,
                    feature_blocks,
                    spin_embed,
                    readout,
                    [state[3] for state in states[1:2]],
                )
            else:
                outputs = mixed_own + mixed_other.astype(jnp.float32)
                slope = (readout_wide * jnp.tanh(outputs)).astype(jnp.bfloat16)
        with jax.named_scope("slope_share"):
            other = partner(slope, 1)
            slopes = [slope, other]
            for k in range(2, mp_size, 2):
                slopes += [partner(slope, k), partner(other, k)]
        with jax.named_scope("derivatives"):
            order = jnp.zeros((1,), jnp.int32) if n else place.reshape(1)
            coded_chunks.append(
                derivative(
                    order,
                    1.0 / unit,
                    normed,
                    bend,
                    down_weight,
                    slopes,
                    samp_size,
                    VMEM_SMALL if n else VMEM_LIMIT,
                )
            )
    with jax.named_scope("derivative_exchange"):
        chunks = [lax.all_to_all(c, SAMPLES, 0, 0) for c in coded_chunks]
        chunks = [c.reshape(-1, rows_dev, hidden_dev) for c in chunks]
    with jax.named_scope("gram"):
        halves, wides = zip(*[rows_first(c) for c in chunks[:-1]])
        gram_part, last_wide = gram_matrix(energy_row, chunks[-1], halves)
        wides = wides + (last_wide,)
    with jax.named_scope("gram_sum"):
        near_size = lax.axis_size(NEAR)
        blocks = lax.all_to_all(
            gram_part.reshape(near_size, sample_count // near_size, sample_count), NEAR, 0, 0
        )
        blocks = share(jnp.sum(blocks, axis=0), FAR)
        shared = share(jnp.sum(blocks, axis=0), NEAR)
    with jax.named_scope("solve"):
        return solve(jnp.concatenate([damping, unit]), shared, wides, rows_dev)


def solution(mesh):
    samples, mp = mesh.devices.shape
    fine = jax.sharding.Mesh(
        mesh.devices.reshape(samples // 4, 2, 2, mp // 2, 2), SAMPLES + MP
    )
    in_specs = (
        P(SAMPLES, None),
        P(SAMPLES, None, None),
        P(),
        P(),
        P(None, MP),
        P(None, MP),
        P(),
        P(SAMPLES),
        P(),
    )
    out_specs = P(SAMPLES, MP)
    return jax.shard_map(body, mesh=fine, in_specs=in_specs, out_specs=out_specs, check_vma=False)
```
